128 devices in a mesh: level: 8 (over z_hi, x), tile: 16 (over z_lo, y, core).
Axes of the slice: x: 4, y: 4, z: 4 (z_hi: 2, z_lo: 2; z = z_hi * 2 + z_lo), core: 2. Of those that a mesh axis runs over, the one named last changes fastest.
Arguments:
- level_state: float32 [8, 16, 256, 2048], P('level', None, 'tile'), may hold values from -2.5 to 2.5
- history: float32 [8, 3, 16, 256, 2048], P('level', None, None, 'tile'), may hold values from -4 to 4
- diffusion: float32 [16], replicated, may hold values from 0.02 to 0.2
- linear_rates: float32 [16, 16], replicated, may hold values from -1.5 to 1.5
- coupling: float32 [16, 16], replicated, may hold values from -1.5 to 1.5
Outputs:
- advanced_state: float32 [8, 16, 256, 2048], P('level', None, 'tile')
The draws below stay inside these ranges and needn't reach their ends.
All inputs are finite; a program needn't handle non-finite values.
Results may differ from the reference program's by a relative error of at most 0.0003.
Values sent between devices are 32-bit elements; how exact they have to be, the bound alone decides.
No kernel may reach another device: no remote copies, remote signals or barrier semaphores. Data moves between devices by JAX's collectives and lax.ppermute only.
A program may use at most 128 MiB of HBM per device.

```python
import math
import jax
import jax.numpy as jnp
from jax import lax

SPECIES = 16
NCOL = 2048
TICKS = 4
LEVELS = 8
NROWS = 256


def draw_level_state(key, part):
    key = jax.random.fold_in(key, 11)
    shape = (LEVELS, SPECIES, NROWS, NCOL)
    return 0.7 * jax.random.truncated_normal(key, -3.0, 3.0, shape, jnp.float32)


def levels(own_key, shape, shards, low, high):
    gain = 1.0
    for position, shards_of in shards:
        heights = jax.random.uniform(jax.random.fold_in(jax.random.fold_in(own_key, 6), position), (shards_of,), jnp.float32, low / len(shards), high / len(shards))
        gain = gain * jnp.repeat(jnp.exp(heights), shape[position] // shards_of).reshape((-1,) + (1,) * (len(shape) - 1 - position))
    return gain


def scatter_about(own_key, shape, width, most, split=(), held_as=jnp.bfloat16):
    loudness = levels(own_key, shape, split, -0.22, 0.18) if split else 1.0
    drawn = jax.random.normal(own_key, shape, jnp.float32) * width * loudness
    return jnp.minimum(jnp.maximum(drawn, -most), most).astype(held_as)


def setup_inputs(seed: int = 0) -> dict:
    keys = jax.random.split(jax.random.key(seed), 6)
    return {
        "level_state": draw_level_state(jax.random.fold_in(keys[5], 71), 0),
        "history": scatter_about(keys[1], (LEVELS, 3, SPECIES, NROWS, NCOL), 1.0, 4.0, ((0, 8), (3, 16)), jnp.float32),
        "diffusion": jnp.clip(jnp.exp(jax.random.uniform(keys[2], (SPECIES,), jnp.float32, math.log(0.02), math.log(0.2))), 0.02, 0.2),
        "linear_rates": scatter_about(keys[3], (SPECIES, SPECIES), SPECIES ** -0.5, 1.5, (), jnp.float32),
        "coupling": scatter_about(keys[4], (SPECIES, SPECIES), SPECIES ** -0.5, 1.5, (), jnp.float32),
    }


STEP_SIZE = 0.4
QUAD_WEIGHTS = (1.0 / 24.0, -5.0 / 24.0, 19.0 / 24.0, 9.0 / 24.0)
DIFF_TAPS = (-1.0 / 12.0, 16.0 / 12.0, -30.0 / 12.0, 16.0 / 12.0, -1.0 / 12.0)


def species_rates(species_field, diffusion, linear_rates, coupling):
    laplace_sum = jnp.zeros_like(species_field)
    for offset in range(5):
        laplace_sum = laplace_sum + DIFF_TAPS[offset] * jnp.roll(species_field, 2 - offset, axis=1)
        laplace_sum = laplace_sum + DIFF_TAPS[offset] * jnp.roll(species_field, 2 - offset, axis=2)
    linear = jnp.einsum("ab,brc->arc", linear_rates, species_field, precision=lax.Precision.HIGHEST)
    saturated = jnp.tanh(jnp.einsum("ab,brc->arc", coupling, species_field, precision=lax.Precision.HIGHEST))
    cubic = species_field * species_field * species_field / 3.0
    return diffusion[:, None, None] * laplace_sum + linear + saturated - cubic


def quadrature(older, middle, newest, current):
    total = QUAD_WEIGHTS[0] * older + QUAD_WEIGHTS[1] * middle
    total = total + (QUAD_WEIGHTS[2] - 1.0) * newest + QUAD_WEIGHTS[3] * current
    return STEP_SIZE * total


def reference(level_state, history, diffusion, linear_rates, coupling):
    older = history[:, 0]
    middle = history[:, 1]
    newest = history[:, 2]
    current_state = level_state
    for step_index in range(TICKS):
        current = lax.map(lambda species_field: species_rates(species_field, diffusion, linear_rates, coupling), current_state)
        outgoing = quadrature(older, middle, newest, current)
        incoming = jnp.concatenate([jnp.zeros_like(outgoing[:1]), outgoing[:-1]], axis=0)
        current_state = current_state + STEP_SIZE * current + incoming
        older, middle, newest = middle, newest, current
    return current_state
```

```python
import functools

import jax
import jax.numpy as jnp
from jax import lax
from jax.experimental import pallas as pl
from jax.experimental.pallas import tpu as pltpu
from jax.sharding import PartitionSpec as P

SPECIES = 16
ROWS = 16
CELLS = SPECIES * ROWS
HALF = CELLS // 2
NCOL = 2048
RING = 4
CHUNK = NCOL // RING
HALO = 8
WIDE = CHUNK + 2 * HALO
EDGE = 2 * SPECIES
STEP = 0.4
W0, W1, W2, W3 = (1.0 / 24.0, -5.0 / 24.0, 19.0 / 24.0, 9.0 / 24.0)
TAPS = (-1.0 / 12.0, 16.0 / 12.0, -30.0 / 12.0, 16.0 / 12.0, -1.0 / 12.0)
SHIFTS = (1, 3, 2)
PAD = 8

f32 = jnp.float32
bf16 = jnp.bfloat16
dot = functools.partial(jnp.dot, preferred_element_type=f32)


def params(mib=24, **kw):
    return pltpu.CompilerParams(vmem_limit_bytes=mib * 1024 * 1024, **kw)


def vmem():
    return pl.BlockSpec(memory_space=pltpu.VMEM)


def hbm():
    return pl.BlockSpec(memory_space=pl.ANY)


def x_shift(by, skip_last=False):
    pairs = []
    for level in range(8):
        if skip_last and level == 7:
            continue
        high, x = divmod(level, RING)
        for tile in range(16):
            pairs.append((level * 16 + tile, (high * RING + (x + by) % RING) * 16 + tile))
    return pairs


def z_up():
    return [((x * 16) + t, ((RING + x) * 16) + t) for x in range(RING) for t in range(16)]


def tile_shift(by):
    return [(l * 16 + t, l * 16 + (t + by) % 16) for l in range(8) for t in range(16)]


def send(value, pairs):
    return lax.ppermute(value, ("level", "tile"), pairs)


def my_x():
    return lax.rem(lax.axis_index("level"), RING)


def my_high():
    return lax.div(lax.axis_index("level"), RING)


def turned(read):
    return jnp.concatenate([read(row) for row in range(ROWS)], axis=0).T


def place(scratch, n, value):
    i = pl.program_id(0)
    at = pl.multiple_of(i * 128, 128) + HALO
    scratch[n, pl.ds(pl.multiple_of(at, 8), 128), :] = value

    @pl.when(i == 0)
    def _():
        scratch[n, NCOL + HALO :, :] = value[:HALO]

    @pl.when(i == NCOL // 128 - 1)
    def _():
        scratch[n, :HALO, :] = value[128 - HALO :]


def hand_out(scratch, outs, sem):
    x = my_x()

    @pl.when(pl.program_id(0) == NCOL // 128 - 1)
    def _():
        copies = []
        for k, out_ref in enumerate(outs):
            n, by = divmod(k, RING)
            base = pl.multiple_of(lax.rem(x + by, RING) * CHUNK, 128)
            copies.append(pltpu.make_async_copy(scratch.at[n, pl.ds(base, WIDE), :], out_ref, sem.at[k]))
        for copy in copies:
            copy.start()
        for copy in copies:
            copy.wait()


def cut_state_kernel(state_ref, *refs):
    outs, scratch, sem = refs[:RING], *refs[RING:]
    place(scratch, 0, turned(lambda row: state_ref[pl.ds(row, SPECIES, stride=ROWS), :]))
    hand_out(scratch, outs, sem)


def cut_history_kernel(older_ref, middle_ref, newest_ref, *refs):
    outs, scratch, sem = refs[: 3 * RING], *refs[3 * RING :]

    def parts(row):
        rows = pl.ds(row, SPECIES, stride=ROWS)
        return older_ref[0, rows, :], middle_ref[0, rows, :], newest_ref[0, rows, :]

    def first(row):
        p, q, r = parts(row)
        return STEP * (W0 * p + W1 * q + (W2 - 1.0) * r)

    def second(row):
        _, q, r = parts(row)
        return STEP * (W0 * q + W1 * r)

    def third(row):
        return (STEP * W0) * parts(row)[2]

    for n, read in enumerate((first, second, third)):
        place(scratch, n, turned(read))
    hand_out(scratch, outs, sem)


def cut_state(state):
    return pl.pallas_call(
        cut_state_kernel,
        grid=(NCOL // 128,),
        out_shape=[jax.ShapeDtypeStruct((WIDE, CELLS), f32)] * RING,
        in_specs=[pl.BlockSpec((CELLS, 128), lambda i: (0, i))],
        out_specs=[hbm()] * RING,
        scratch_shapes=[pltpu.VMEM((1, NCOL + 2 * HALO, CELLS), f32), pltpu.SemaphoreType.DMA((RING,))],
        compiler_params=params(),
        name="cut_state",
    )(state)


def cut_history(hist):
    part = lambda n: pl.BlockSpec((1, CELLS, 128), lambda i: (n, 0, i))
    return pl.pallas_call(
        cut_history_kernel,
        grid=(NCOL // 128,),
        out_shape=[jax.ShapeDtypeStruct((WIDE, CELLS), f32)] * (3 * RING),
        in_specs=[part(0), part(1), part(2)],
        out_specs=[hbm()] * (3 * RING),
        scratch_shapes=[pltpu.VMEM((3, NCOL + 2 * HALO, CELLS), f32), pltpu.SemaphoreType.DMA((3 * RING,))],
        compiler_params=params(),
        name="cut_history",
    )(hist, hist, hist)


def update_kernel(step, *refs):
    refs = list(refs)
    take = lambda n: [refs.pop(0) for _ in range(n)]
    new_field = take(RING) if step < 4 else None
    old_field = take(RING) if step > 0 else None
    y_ref, g_ref = take(2) if step > 0 else (None, None)
    z_ref = take(1)[0] if step > 1 else None
    u_ref, down_ref, up_ref = take(3)
    pay_ref = take(1)[0] if step > 0 else None
    x, high = my_x(), my_high()
    level_of = lambda by: lax.rem(x + RING - by, RING)

    def plain(field):
        for by in range(RING):
            u_ref[level_of(by)] = field[by][...]

    def added(field, with_pay):
        for by in range(RING):
            level = level_of(by)

            @pl.when(level < RING - 1)
            def _(by=by, level=level):
                u_ref[level + 1] = y_ref[level + 1] + field[by][...]

            if with_pay:

                @pl.when(level == RING - 1)
                def _(by=by):
                    pay_ref[...] = g_ref[...] + field[by][...]

    @pl.when(high == 0)
    def _():
        if step == 0:
            plain(new_field)
        elif step < 4:
            u_ref[0] = y_ref[0]
            added(new_field, True)
        else:
            u_ref[...] = y_ref[...]
            pay_ref[...] = g_ref[...]

    @pl.when(high == 1)
    def _():
        if step == 0:
            u_ref[...] = jnp.zeros_like(u_ref)
        elif step == 1:
            plain(old_field)
        else:
            u_ref[0] = y_ref[0] + z_ref[...]
            added(old_field, False)
        if step > 0:
            pay_ref[...] = jnp.zeros_like(pay_ref)

    lane = lax.broadcasted_iota(jnp.int32, (WIDE, HALF), 1)
    down = up = None
    for level in range(RING):
        here = (lane >= level * EDGE) & (lane < (level + 1) * EDGE)
        top = u_ref[level, :, :HALF]
        bottom = u_ref[level, :, HALF:]
        top = pltpu.roll(top, level * EDGE, 1) if level else top
        bottom = pltpu.roll(bottom, (level + 1) * EDGE, 1) if level < RING - 1 else bottom
        down = top if level == 0 else jnp.where(here, top, down)
        up = bottom if level == 0 else jnp.where(here, bottom, up)
    down_ref[...] = down
    up_ref[...] = up


def update(step, new_field, old_field, y, g, z):
    operands = []
    if step < 4:
        operands += new_field
    if step > 0:
        operands += old_field + [y, g]
    if step > 1:
        operands.append(z)
    outs = [pltpu.VMEM((RING, WIDE, CELLS), f32)] + [jax.ShapeDtypeStruct((WIDE, HALF), f32)] * 2
    if step > 0:
        outs.append(jax.ShapeDtypeStruct((WIDE, CELLS), f32))
    return pl.pallas_call(
        functools.partial(update_kernel, step),
        out_shape=outs,
        in_specs=[vmem()] * len(operands),
        out_specs=[vmem()] * len(outs),
        compiler_params=params(),
        name=f"update_{step}",
    )(*operands)


def rates_kernel(step, n_in, n_out, u_ref, above_ref, below_ref, main_ref, edge_ref, diff_ref, *refs):
    older = refs[:n_in]
    y_ref, g_ref = refs[n_in : n_in + 2]
    newer = refs[n_in + 2 : n_in + 2 + n_out]
    padded, stack, edges = refs[n_in + 2 + n_out :]

    def split(into, at, value):
        high_part = value.astype(bf16)
        width = value.shape[1]
        into[:, at : at + width] = high_part
        into[:, CELLS + at : CELLS + at + width] = (value - high_part.astype(f32)).astype(bf16)
        into[:, 2 * CELLS + at : 2 * CELLS + at + width] = high_part

    def work():
        padded[:, :PAD, :] = jnp.zeros((2, PAD, HALF), f32)
        padded[:, PAD + WIDE :, :] = jnp.zeros((2, PAD, HALF), f32)
        split(stack, 0, above_ref[...])
        split(stack, HALF, below_ref[...])
        edges[...] = dot(stack[...], edge_ref[...])
        g_ref[...] = jnp.zeros_like(g_ref)
        for level in range(RING):
            for side in range(2):
                part = u_ref[level, :, side * HALF : (side + 1) * HALF]
                padded[side, PAD : PAD + WIDE, :] = part
                split(stack, side * HALF, part)
            products = dot(stack[...], main_ref[...])
            for side in range(2):
                at = slice(side * HALF, (side + 1) * HALF)
                lane = lax.broadcasted_iota(jnp.int32, (48, HALF), 1)
                near_edge = lane >= HALF - EDGE if side else lane < EDGE
                turn = (HALF - EDGE - level * EDGE if side else HALF - level * EDGE) % HALF
                diff = diff_ref[0:1, at]
                for begin in range(0, WIDE, 48):
                    rows = slice(begin, begin + 48)
                    moved = lambda by: padded[side, PAD + begin + by : PAD + begin + by + 48, :]
                    u = moved(0)
                    near = moved(-1) + moved(1)
                    far = moved(-2) + moved(2)
                    edge = edges[rows, at]
                    edge = pltpu.roll(edge, turn, 1) if turn else edge
                    rate = products[rows, at] + jnp.where(near_edge, edge, 0.0)
                    rate = rate + diff * (16.0 * near - far)
                    rate = rate + jnp.tanh(products[rows, CELLS + side * HALF : CELLS + (side + 1) * HALF])
                    scaled = STEP * (rate - u * u * u * (1.0 / 3.0))
                    y_ref[level, rows, at] = u + scaled + g_ref[rows, at]
                    out = W3 * scaled
                    if n_in > 0:
                        out = out + older[0][level, rows, at]
                    g_ref[rows, at] = out
                    for k, weight in zip(range(n_out), (W2 - 1.0, W1, W0)):
                        value = weight * scaled
                        if k + 1 < n_in:
                            value = value + older[k + 1][level, rows, at]
                        newer[k][level, rows, at] = value

    if step < 4:
        work()
    else:
        high = my_high()
        pl.when(high == 1)(work)

        @pl.when(high == 0)
        def _():
            y_ref[...] = u_ref[...]
            g_ref[...] = jnp.zeros_like(g_ref)


def rates(step, u, above, below, weights, older, n_out):
    n_in = len(older)
    full = pltpu.VMEM((RING, WIDE, CELLS), f32)
    outs = pl.pallas_call(
        functools.partial(rates_kernel, step, n_in, n_out),
        out_shape=[full, pltpu.VMEM((WIDE, CELLS), f32)] + [full] * n_out,
        in_specs=[vmem()] * (6 + n_in),
        out_specs=[vmem()] * (2 + n_out),
        scratch_shapes=[
            pltpu.VMEM((2, WIDE + 2 * PAD, HALF), f32),
            pltpu.VMEM((WIDE, 3 * CELLS), bf16),
            pltpu.VMEM((WIDE, CELLS), f32),
        ],
        compiler_params=params(),
        name=f"rates_{step}",
    )(u, above, below, *weights, *older)
    return outs[0], outs[1], list(outs[2:])


def weights_kernel(lin_ref, coup_ref, diff_ref, main_ref, edge_ref, diff_out):
    exact = functools.partial(lax.dot_general, precision=lax.Precision.HIGHEST, preferred_element_type=f32)
    last = (((1,), (1,)), ((), ()))
    iota = lambda shape, dim: lax.broadcasted_iota(jnp.int32, shape, dim)
    pick = (iota((CELLS, SPECIES), 0) % SPECIES == iota((CELLS, SPECIES), 1)).astype(f32)
    source, target = iota((CELLS, CELLS), 0), iota((CELLS, CELLS), 1)
    same_row = source // SPECIES == target // SPECIES
    same_species = source % SPECIES == target % SPECIES
    diffusion = exact(diff_ref[...], pick, last)

    def tiled(matrix):
        return jnp.where(same_row, exact(exact(pick, matrix, last), pick, last), 0.0)

    def stencil(offset, middle):
        value = jnp.where(offset == 0, middle, 0.0)
        value = value + jnp.where((offset == 1) | (offset == -1), TAPS[1], 0.0)
        return value + jnp.where((offset == 2) | (offset == -2), TAPS[0], 0.0)

    def put(into, at, value):
        high_part = value.astype(bf16)
        into[:CELLS, at : at + CELLS] = high_part
        into[CELLS : 2 * CELLS, at : at + CELLS] = high_part
        into[2 * CELLS :, at : at + CELLS] = (value - high_part.astype(f32)).astype(bf16)

    offset = source // SPECIES - target // SPECIES
    spread = jnp.where(same_species, stencil(offset, 2.0 * TAPS[2]) * diffusion[0:1], 0.0)
    put(main_ref, 0, tiled(lin_ref[...]) + spread)
    put(main_ref, CELLS, tiled(coup_ref[...]))
    row_from = (source // SPECIES) % 2 + jnp.where(source < HALF, -2, ROWS)
    row_to = (target // SPECIES) % 2 + jnp.where(target < HALF, 0, ROWS - 2)
    alike = same_species & (source // EDGE == target // EDGE)
    put(edge_ref, 0, jnp.where(alike, stencil(row_from - row_to, 0.0) * diffusion[0:1], 0.0))
    diff_out[...] = diffusion * (1.0 / 12.0)


def make_weights(diffusion, linear_rates, coupling):
    return pl.pallas_call(
        weights_kernel,
        out_shape=[
            pltpu.VMEM((3 * CELLS, 2 * CELLS), bf16),
            pltpu.VMEM((3 * CELLS, CELLS), bf16),
            pltpu.VMEM((8, CELLS), f32),
        ],
        in_specs=[vmem()] * 3,
        out_specs=[vmem()] * 3,
        compiler_params=params(),
        name="weights",
    )(linear_rates, coupling, jnp.broadcast_to(diffusion[None], (8, SPECIES)))


def finish_kernel(y_ref, z_ref, *outs):
    x, high = my_x(), my_high()
    inner = slice(HALO, HALO + CHUNK)
    for by, out_ref in enumerate(outs):
        level = lax.rem(x + by, RING)
        takes = (level == 0) & (high == 1)

        @pl.when(takes)
        def _(out_ref=out_ref):
            out_ref[...] = y_ref[0, inner, :] + z_ref[inner, :]

        @pl.when(jnp.logical_not(takes))
        def _(out_ref=out_ref, level=level):
            out_ref[...] = y_ref[level, inner, :]


def finish(y, z):
    return pl.pallas_call(
        finish_kernel,
        out_shape=[jax.ShapeDtypeStruct((CHUNK, CELLS), f32)] * RING,
        in_specs=[vmem(), vmem()],
        out_specs=[vmem()] * RING,
        compiler_params=params(),
        name="finish",
    )(y, z)


def join_kernel(x_ref, *refs):
    parts, out_ref = refs[:RING], refs[RING]
    by = pl.program_id(0)
    for k, part in enumerate(parts):

        @pl.when(by == k)
        def _(part=part):
            value = part[...].T
            for row in range(ROWS):
                out_ref[pl.ds(row, SPECIES, stride=ROWS), :] = value[row * SPECIES : (row + 1) * SPECIES]


def join(parts, x):
    blocks = CHUNK // 128

    def spec(k):
        return pl.BlockSpec(
            (128, CELLS), lambda by, i, x_ref: (jnp.where(by == k, i, jnp.where(by < k, 0, blocks - 1)), 0)
        )

    return pl.pallas_call(
        join_kernel,
        grid_spec=pltpu.PrefetchScalarGridSpec(
            num_scalar_prefetch=1,
            grid=(RING, blocks),
            in_specs=[spec(k) for k in range(RING)],
            out_specs=pl.BlockSpec(
                (CELLS, 128), lambda by, i, x_ref: (0, lax.rem(x_ref[0] + RING - by, RING) * blocks + i)
            ),
        ),
        out_shape=jax.ShapeDtypeStruct((CELLS, NCOL), f32),
        compiler_params=params(dimension_semantics=("arbitrary", "arbitrary")),
        name="join",
    )(x, *parts)


def exchange(parts, earlier, skip_last=False):
    got = [parts[0], None, None, None]
    for by in SHIFTS:
        part = parts[by]
        if earlier is not None:
            part, _ = lax.optimization_barrier((part, earlier[by]))
        got[by] = send(part, x_shift(by, skip_last))
    return got


def local(level_state, history, diffusion, linear_rates, coupling):
    state = level_state.reshape(CELLS, NCOL)
    hist = history.reshape(3, CELLS, NCOL)
    weights = make_weights(diffusion, linear_rates, coupling)
    cut = cut_history(hist)
    fields = [exchange(cut_state(state), None)]
    for f in range(3):
        fields.append(exchange(cut[f * RING : (f + 1) * RING], fields[-1], True))

    y = g = z = None
    older = []
    n_outs = (3, 3, 2, 1, 0)
    for step in range(5):
        new_field = fields[step] if step < 4 else None
        old_field = fields[step - 1] if step > 0 else None
        u, down, up, *pay = update(step, new_field, old_field, y, g, z)
        above = send(up, tile_shift(1))
        below = send(down, tile_shift(-1))
        z = send(pay[0], z_up()) if pay else None
        y, g, older = rates(step, u, above, below, weights, older, n_outs[step])
    parts = finish(y, z)
    out = join(exchange(parts, None), my_x()[None])
    return out.reshape(1, SPECIES, ROWS, NCOL)


def solution(mesh):
    placed = (P("level", None, "tile", None), P("level", None, None, "tile", None), P(), P(), P())
    return jax.shard_map(
        local, mesh=mesh, in_specs=placed, out_specs=P("level", None, "tile", None), check_vma=False
    )
```

```python
import functools

import jax
import jax.numpy as jnp
from jax import lax
from jax.experimental import pallas as pl
from jax.experimental.pallas import tpu as pltpu
from jax.sharding import PartitionSpec as P

SPECIES = 16
ROWS = 16
CELLS = SPECIES * ROWS
HALF = CELLS // 2
NCOL = 2048
RING = 4
CHUNK = NCOL // RING
HALO = 8
WIDE = CHUNK + 2 * HALO
EDGE = 2 * SPECIES
STEP = 0.4
W0, W1, W2, W3 = (1.0 / 24.0, -5.0 / 24.0, 19.0 / 24.0, 9.0 / 24.0)
TAPS = (-1.0 / 12.0, 16.0 / 12.0, -30.0 / 12.0, 16.0 / 12.0, -1.0 / 12.0)
SHIFTS = (1, 3, 2)
PAD = 8

LONG = pl.CostEstimate(flops=10**10, bytes_accessed=10**8, transcendentals=0)

f32 = jnp.float32
bf16 = jnp.bfloat16
dot = functools.partial(jnp.dot, preferred_element_type=f32)


def params(mib=24, **kw):
    return pltpu.CompilerParams(vmem_limit_bytes=mib * 1024 * 1024, **kw)


def vmem():
    return pl.BlockSpec(memory_space=pltpu.VMEM)


def hbm():
    return pl.BlockSpec(memory_space=pl.ANY)


def x_swap(by, skip_last=False):
    pairs = []
    for level in range(8):
        if skip_last and level == 7:
            continue
        for tile in range(16):
            pairs.append((level * 16 + tile, (level ^ by) * 16 + tile))
    return pairs


def z_up():
    return [((x * 16) + t, ((RING + x) * 16) + t) for x in range(RING) for t in range(16)]


def core_swap():
    return [(l * 16 + t, l * 16 + (t ^ 1)) for l in range(8) for t in range(16)]


def chip_swap():
    return [(l * 16 + t, l * 16 + (t + (1 if t % 2 else 15)) % 16) for l in range(8) for t in range(16)]


def send(value, pairs):
    return lax.ppermute(value, ("level", "tile"), pairs)


def send_up(value, pieces):
    rows = value.shape[0] // pieces
    return [send(value[i * rows : (i + 1) * rows], z_up()) for i in range(pieces)]


def my_x():
    return lax.rem(lax.axis_index("level"), RING)


def my_core():
    return lax.rem(lax.axis_index("tile"), 2)


def my_high():
    return lax.div(lax.axis_index("level"), RING)


def turned(read):
    return jnp.concatenate([read(row) for row in range(ROWS)], axis=0).T


def place(scratch, n, value):
    i = pl.program_id(0)
    at = pl.multiple_of(i * 128, 128) + HALO
    scratch[n, pl.ds(pl.multiple_of(at, 8), 128), :] = value

    @pl.when(i == 0)
    def _():
        scratch[n, NCOL + HALO :, :] = value[:HALO]

    @pl.when(i == NCOL // 128 - 1)
    def _():
        scratch[n, :HALO, :] = value[128 - HALO :]


def hand_out(scratch, outs, sem):
    x = my_x()

    @pl.when(pl.program_id(0) == NCOL // 128 - 1)
    def _():
        copies = []
        for k, (n, by, out_ref) in enumerate(outs):
            base = pl.multiple_of(lax.bitwise_xor(x, by) * CHUNK, 128)
            copies.append(pltpu.make_async_copy(scratch.at[n, pl.ds(base, WIDE), :], out_ref, sem.at[k]))
        for copy in copies:
            copy.start()
        for copy in copies:
            copy.wait()


def cut_state_kernel(state_ref, *refs):
    outs, scratch, sem = refs[:RING], *refs[RING:]
    place(scratch, 0, turned(lambda row: state_ref[pl.ds(row, SPECIES, stride=ROWS), :]))
    hand_out(scratch, [(0, by, out_ref) for by, out_ref in enumerate(outs)], sem)


def cut_history_kernel(older_ref, middle_ref, newest_ref, *refs):
    pairs, lasts, (scratch, sem) = refs[:RING], refs[RING : 2 * RING], refs[2 * RING :]

    def parts(row):
        rows = pl.ds(row, SPECIES, stride=ROWS)
        return older_ref[0, rows, :], middle_ref[0, rows, :], newest_ref[0, rows, :]

    def first(row):
        p, q, r = parts(row)
        return STEP * (W0 * p + W1 * q + (W2 - 1.0) * r)

    def second(row):
        _, q, r = parts(row)
        return STEP * (W0 * q + W1 * r)

    def third(row):
        return (STEP * W0) * parts(row)[2]

    for n, read in enumerate((first, second, third)):
        place(scratch, n, turned(read))
    pieces = [(n, by, pairs[by].at[n * WIDE : (n + 1) * WIDE]) for n in range(2) for by in range(RING)]
    hand_out(scratch, pieces + [(2, by, lasts[by]) for by in range(RING)], sem)


def cut_state(state):
    return pl.pallas_call(
        cut_state_kernel,
        grid=(NCOL // 128,),
        out_shape=[jax.ShapeDtypeStruct((WIDE, CELLS), f32)] * RING,
        in_specs=[pl.BlockSpec((CELLS, 128), lambda i: (0, i))],
        out_specs=[hbm()] * RING,
        scratch_shapes=[pltpu.VMEM((1, NCOL + 2 * HALO, CELLS), f32), pltpu.SemaphoreType.DMA((RING,))],
        compiler_params=params(),
        name="cut_state",
    )(state)


def cut_history(hist):
    part = lambda n: pl.BlockSpec((1, CELLS, 128), lambda i: (n, 0, i))
    return pl.pallas_call(
        cut_history_kernel,
        grid=(NCOL // 128,),
        out_shape=[jax.ShapeDtypeStruct((2 * WIDE, CELLS), f32)] * RING
        + [jax.ShapeDtypeStruct((WIDE, CELLS), f32)] * RING,
        in_specs=[part(0), part(1), part(2)],
        out_specs=[hbm()] * (2 * RING),
        scratch_shapes=[pltpu.VMEM((3, NCOL + 2 * HALO, CELLS), f32), pltpu.SemaphoreType.DMA((3 * RING,))],
        compiler_params=params(),
        name="cut_history",
    )(hist, hist, hist)


def update_kernel(step, starts, pieces, *refs):
    refs = list(refs)
    take = lambda n: [refs.pop(0) for _ in range(n)]
    new_field = take(RING) if step < 4 else None
    old_field = take(RING) if step > 0 else None
    piece = lambda field, k: field[starts[k] : starts[k] + WIDE, :]
    y_ref, g_ref = take(2) if step > 0 else (None, None)
    z_refs = take(pieces) if step > 1 else None
    u_ref, inner_ref, outer_ref = take(3)
    pay_ref = take(1)[0] if 0 < step < 4 else None
    x, high = my_x(), my_high()
    level_of = lambda by: lax.bitwise_xor(x, by)

    def plain(field, k):
        for by in range(RING):
            u_ref[level_of(by)] = piece(field[by], k)

    def added(field, k, with_pay):
        for by in range(RING):
            level = level_of(by)

            @pl.when(level < RING - 1)
            def _(by=by, level=level):
                u_ref[level + 1] = y_ref[level + 1] + piece(field[by], k)

            if with_pay:

                @pl.when(level == RING - 1)
                def _(by=by):
                    pay_ref[...] = g_ref[...] + piece(field[by], k)

    @pl.when(high == 0)
    def _():
        if step == 0:
            plain(new_field, 0)
        elif step < 4:
            u_ref[0] = y_ref[0]
            added(new_field, 0, True)
        else:
            u_ref[...] = y_ref[...]

    @pl.when(high == 1)
    def _():
        if step == 0:
            u_ref[...] = jnp.zeros_like(u_ref)
        elif step == 1:
            plain(old_field, 1)
        else:
            for i, z_ref in enumerate(z_refs):
                rows = slice(i * (WIDE // pieces), (i + 1) * (WIDE // pieces))
                u_ref[0, rows, :] = y_ref[0, rows, :] + z_ref[...]
            added(old_field, 1, False)
        if 0 < step < 4:
            pay_ref[...] = jnp.zeros_like(pay_ref)

    lane = lax.broadcasted_iota(jnp.int32, (WIDE, HALF), 1)
    down = up = None
    for level in range(RING):
        here = (lane >= level * EDGE) & (lane < (level + 1) * EDGE)
        top = u_ref[level, :, :HALF]
        bottom = u_ref[level, :, HALF:]
        top = pltpu.roll(top, level * EDGE, 1) if level else top
        bottom = pltpu.roll(bottom, (level + 1) * EDGE, 1) if level < RING - 1 else bottom
        down = top if level == 0 else jnp.where(here, top, down)
        up = bottom if level == 0 else jnp.where(here, bottom, up)
    first_core = my_core() == 0
    inner_ref[...] = jnp.where(first_core, up, down)
    outer_ref[...] = jnp.where(first_core, down, up)


def update(step, new_field, old_field, y, g, z):
    operands, starts = [], [0, 0]
    if step < 4:
        operands += new_field[0]
        starts[0] = new_field[1]
    if step > 0:
        operands += old_field[0] + [y, g]
        starts[1] = old_field[1]
    if step > 1:
        operands += z
    outs = [pltpu.VMEM((RING, WIDE, CELLS), f32)] + [jax.ShapeDtypeStruct((WIDE, HALF), f32)] * 2
    if 0 < step < 4:
        outs.append(jax.ShapeDtypeStruct((WIDE, CELLS), f32))
    return pl.pallas_call(
        functools.partial(update_kernel, step, starts, len(z) if z else 0),
        out_shape=outs,
        in_specs=[vmem()] * len(operands),
        out_specs=[vmem()] * len(outs),
        cost_estimate=LONG,
        compiler_params=params(),
        name=f"update_{step}",
    )(*operands)


def split(into, at, value):
    high_part = value.astype(bf16)
    width = value.shape[1]
    into[:, at : at + width] = high_part
    into[:, CELLS + at : CELLS + at + width] = (value - high_part.astype(f32)).astype(bf16)
    into[:, 2 * CELLS + at : 2 * CELLS + at + width] = high_part


def unless_done(step, work):
    if step < 4:
        work()
    else:
        pl.when(my_high() == 1)(work)


def inner_kernel(step, u_ref, main_ref, diff_ref, rate_ref, padded, stack):
    def work():
        padded[:, :PAD, :] = jnp.zeros((2, PAD, HALF), f32)
        padded[:, PAD + WIDE :, :] = jnp.zeros((2, PAD, HALF), f32)
        for level in range(RING):
            for side in range(2):
                part = u_ref[level, :, side * HALF : (side + 1) * HALF]
                padded[side, PAD : PAD + WIDE, :] = part
                split(stack, side * HALF, part)
            products = dot(stack[...], main_ref[...])
            for side in range(2):
                at = slice(side * HALF, (side + 1) * HALF)
                diff = diff_ref[0:1, at]
                for begin in range(0, WIDE, 48):
                    rows = slice(begin, begin + 48)
                    moved = lambda by: padded[side, PAD + begin + by : PAD + begin + by + 48, :]
                    u = moved(0)
                    near = moved(-1) + moved(1)
                    far = moved(-2) + moved(2)
                    rate = products[rows, at] + diff * (16.0 * near - far)
                    rate = rate + jnp.tanh(products[rows, CELLS + side * HALF : CELLS + (side + 1) * HALF])
                    rate_ref[level, rows, at] = rate - u * u * u * (1.0 / 3.0)

    unless_done(step, work)


def inner_rates(step, u, weights):
    main, _, diff = weights
    return pl.pallas_call(
        functools.partial(inner_kernel, step),
        out_shape=pltpu.VMEM((RING, WIDE, CELLS), f32),
        in_specs=[vmem()] * 3,
        out_specs=vmem(),
        scratch_shapes=[pltpu.VMEM((2, WIDE + 2 * PAD, HALF), f32), pltpu.VMEM((WIDE, 3 * CELLS), bf16)],
        compiler_params=params(),
        name=f"inner_{step}",
    )(u, main, diff)


def rates_kernel(step, n_in, n_out, u_ref, rate_ref, inner_ref, outer_ref, edge_ref, *refs):
    older = refs[:n_in]
    y_ref, g_ref = refs[n_in : n_in + 2]
    newer = refs[n_in + 2 : n_in + 2 + n_out]
    stack, edges = refs[n_in + 2 + n_out :]

    def work():
        first_core = my_core() == 0
        split(stack, 0, jnp.where(first_core, outer_ref[...], inner_ref[...]))
        split(stack, HALF, jnp.where(first_core, inner_ref[...], outer_ref[...]))
        edges[...] = dot(stack[...], edge_ref[...])
        lane = lax.broadcasted_iota(jnp.int32, (48, HALF), 1)
        for side in range(2):
            at = slice(side * HALF, (side + 1) * HALF)
            near_edge = lane >= HALF - EDGE if side else lane < EDGE
            for begin in range(0, WIDE, 48):
                rows = slice(begin, begin + 48)
                below = None
                for level in range(RING):
                    turn = (HALF - EDGE - level * EDGE if side else HALF - level * EDGE) % HALF
                    edge = edges[rows, at]
                    edge = pltpu.roll(edge, turn, 1) if turn else edge
                    scaled = STEP * (rate_ref[level, rows, at] + jnp.where(near_edge, edge, 0.0))
                    y = u_ref[level, rows, at] + scaled
                    y_ref[level, rows, at] = y if below is None else y + below
                    below = W3 * scaled
                    if n_in > 0:
                        below = below + older[0][level, rows, at]
                    for k, weight in zip(range(n_out), (W2 - 1.0, W1, W0)):
                        value = weight * scaled
                        if k + 1 < n_in:
                            value = value + older[k + 1][level, rows, at]
                        newer[k][level, rows, at] = value
                g_ref[rows, at] = below

    unless_done(step, work)
    if step == 4:

        @pl.when(my_high() == 0)
        def _():
            y_ref[...] = u_ref[...]
            g_ref[...] = jnp.zeros_like(g_ref)


def rates(step, u, rate, inner, outer, weights, older, n_out):
    n_in = len(older)
    full = pltpu.VMEM((RING, WIDE, CELLS), f32)
    outs = pl.pallas_call(
        functools.partial(rates_kernel, step, n_in, n_out),
        out_shape=[full, pltpu.VMEM((WIDE, CELLS), f32)] + [full] * n_out,
        in_specs=[vmem()] * (5 + n_in),
        out_specs=[vmem()] * (2 + n_out),
        scratch_shapes=[pltpu.VMEM((WIDE, 3 * CELLS), bf16), pltpu.VMEM((WIDE, CELLS), f32)],
        compiler_params=params(),
        name=f"rates_{step}",
    )(u, rate, inner, outer, weights[1], *older)
    return outs[0], outs[1], list(outs[2:])


def weights_kernel(lin_ref, coup_ref, diff_ref, main_ref, edge_ref, diff_out):
    exact = functools.partial(lax.dot_general, precision=lax.Precision.HIGHEST, preferred_element_type=f32)
    last = (((1,), (1,)), ((), ()))
    iota = lambda shape, dim: lax.broadcasted_iota(jnp.int32, shape, dim)
    pick = (iota((CELLS, SPECIES), 0) % SPECIES == iota((CELLS, SPECIES), 1)).astype(f32)
    source, target = iota((CELLS, CELLS), 0), iota((CELLS, CELLS), 1)
    same_row = source // SPECIES == target // SPECIES
    same_species = source % SPECIES == target % SPECIES
    diffusion = exact(diff_ref[...], pick, last)

    def tiled(matrix):
        return jnp.where(same_row, exact(exact(pick, matrix, last), pick, last), 0.0)

    def stencil(offset, middle):
        value = jnp.where(offset == 0, middle, 0.0)
        value = value + jnp.where((offset == 1) | (offset == -1), TAPS[1], 0.0)
        return value + jnp.where((offset == 2) | (offset == -2), TAPS[0], 0.0)

    def put(into, at, value):
        high_part = value.astype(bf16)
        into[:CELLS, at : at + CELLS] = high_part
        into[CELLS : 2 * CELLS, at : at + CELLS] = high_part
        into[2 * CELLS :, at : at + CELLS] = (value - high_part.astype(f32)).astype(bf16)

    offset = source // SPECIES - target // SPECIES
    spread = jnp.where(same_species, stencil(offset, 2.0 * TAPS[2]) * diffusion[0:1], 0.0)
    put(main_ref, 0, tiled(lin_ref[...]) + spread)
    put(main_ref, CELLS, tiled(coup_ref[...]))
    row_from = (source // SPECIES) % 2 + jnp.where(source < HALF, -2, ROWS)
    row_to = (target // SPECIES) % 2 + jnp.where(target < HALF, 0, ROWS - 2)
    alike = same_species & (source // EDGE == target // EDGE)
    put(edge_ref, 0, jnp.where(alike, stencil(row_from - row_to, 0.0) * diffusion[0:1], 0.0))
    diff_out[...] = diffusion * (1.0 / 12.0)


def make_weights(diffusion, linear_rates, coupling):
    return pl.pallas_call(
        weights_kernel,
        out_shape=[
            pltpu.VMEM((3 * CELLS, 2 * CELLS), bf16),
            pltpu.VMEM((3 * CELLS, CELLS), bf16),
            pltpu.VMEM((8, CELLS), f32),
        ],
        in_specs=[vmem()] * 3,
        out_specs=[vmem()] * 3,
        compiler_params=params(),
        name="weights",
    )(linear_rates, coupling, jnp.broadcast_to(diffusion[None], (8, SPECIES)))


def finish_kernel(y_ref, z_ref, *outs):
    x, high = my_x(), my_high()
    inner = slice(HALO, HALO + CHUNK)
    for by, out_ref in enumerate(outs):
        level = lax.bitwise_xor(x, by)
        takes = (level == 0) & (high == 1)

        @pl.when(takes)
        def _(out_ref=out_ref):
            out_ref[...] = y_ref[0, inner, :] + z_ref[inner, :]

        @pl.when(jnp.logical_not(takes))
        def _(out_ref=out_ref, level=level):
            out_ref[...] = y_ref[level, inner, :]


def finish(y, z):
    return pl.pallas_call(
        finish_kernel,
        out_shape=[jax.ShapeDtypeStruct((CHUNK, CELLS), f32)] * RING,
        in_specs=[vmem(), vmem()],
        out_specs=[vmem()] * RING,
        compiler_params=params(),
        name="finish",
    )(y, z)


def join_kernel(*refs):
    parts, (out_ref, turn, whole, sem) = refs[:RING], refs[RING:]
    x = my_x()
    copies = []
    for half in range(2):
        for by, part in enumerate(parts):
            base = lax.bitwise_xor(x, by) * CHUNK
            for i in range(CHUNK // 128):
                slot = by * (CHUNK // 128) + i
                turn[slot] = part[i * 128 : (i + 1) * 128, half * HALF : (half + 1) * HALF].T
                columns = pl.ds(pl.multiple_of(base + i * 128, 128), 128)
                for species in range(SPECIES):
                    whole[half, species, :, columns] = turn[slot, pl.ds(species, ROWS // 2, stride=SPECIES), :]
        target = out_ref.at[:, half * (ROWS // 2) : (half + 1) * (ROWS // 2), :]
        copies.append(pltpu.make_async_copy(whole.at[half], target, sem.at[half]))
        copies[-1].start()
    for copy in copies:
        copy.wait()


def join(parts):
    return pl.pallas_call(
        join_kernel,
        out_shape=jax.ShapeDtypeStruct((SPECIES, ROWS, NCOL), f32),
        in_specs=[vmem()] * RING,
        out_specs=hbm(),
        scratch_shapes=[
            pltpu.VMEM((NCOL // 128, HALF, 128), f32),
            pltpu.VMEM((2, SPECIES, ROWS // 2, NCOL), f32),
            pltpu.SemaphoreType.DMA((2,)),
        ],
        compiler_params=params(),
        name="join",
    )(*parts)


def after(value, *earlier):
    return lax.optimization_barrier((value, *earlier))[0]


def exchange(parts, skip_last=False):
    got = [parts[0], None, None, None]
    for by in SHIFTS:
        got[by] = send(parts[by], x_swap(by, skip_last))
    return got


def local(level_state, history, diffusion, linear_rates, coupling):
    state = level_state.reshape(CELLS, NCOL)
    hist = history.reshape(3, CELLS, NCOL)
    weights = make_weights(diffusion, linear_rates, coupling)
    cut = cut_history(hist)
    first = exchange(cut_state(state))
    pair = exchange([after(part, *first[1:]) for part in cut[:RING]], True)
    last = [after(part, *pair[1:]) for part in cut[RING:]]
    got = {by: send(last[by], x_swap(by, True)) for by in (1, 3)}
    got[2] = send(after(last[2], got[1], got[3]), x_swap(2, True))
    last = [last[0], got[1], got[2], got[3]]
    fields = [(first, 0), (pair, 0), (pair, WIDE), (last, 0)]

    y = g = z = None
    older = []
    n_outs = (3, 3, 2, 1, 0)
    for step in range(5):
        new_field = fields[step] if step < 4 else None
        old_field = fields[step - 1] if step > 0 else None
        if step == 2:
            y = after(y, last[1], last[3])
        u, inner, outer, *pay = update(step, new_field, old_field, y, g, z)
        outer = send(outer, chip_swap())
        inner = send(inner, core_swap())
        if pay:
            z = send_up(pay[0], 1)
        if step == 2:
            u = after(u, last[2])
        rate = inner_rates(step, u, weights)
        y, g, older = rates(step, u, rate, inner, outer, weights, older, n_outs[step])
        if step == 3:
            z_last = send_up(g, 1)
    parts = finish(y, z_last[0])
    return join(exchange(parts))[None]


def solution(mesh):
    placed = (P("level", None, "tile", None), P("level", None, None, "tile", None), P(), P(), P())
    return jax.shard_map(
        local, mesh=mesh, in_specs=placed, out_specs=P("level", None, "tile", None), check_vma=False
    )
```

```python
import functools

import jax
import jax.numpy as jnp
from jax import lax
from jax.experimental import pallas as pl
from jax.experimental.pallas import tpu as pltpu
from jax.sharding import PartitionSpec as P

SPECIES = 16
ROWS = 16
CELLS = SPECIES * ROWS
HALF = CELLS // 2
NCOL = 2048
LEVELS = 8
CHUNK = NCOL // LEVELS
HALO = 8
WIDE = CHUNK + 2 * HALO
EDGE = 2 * SPECIES
STEP = 0.4
W0, W1, W2, W3 = (1.0 / 24.0, -5.0 / 24.0, 19.0 / 24.0, 9.0 / 24.0)
TAPS = (-1.0 / 12.0, 16.0 / 12.0, -30.0 / 12.0, 16.0 / 12.0, -1.0 / 12.0)
PAD = 8
FIELDS = 4
GROUP = HALF // EDGE
BAND = WIDE // 2

f32 = jnp.float32
bf16 = jnp.bfloat16
dot = functools.partial(jnp.dot, preferred_element_type=f32)


def params(mib=24, **kw):
    return pltpu.CompilerParams(vmem_limit_bytes=mib * 1024 * 1024, **kw)


def vmem():
    return pl.BlockSpec(memory_space=pltpu.VMEM)


def hbm():
    return pl.BlockSpec(memory_space=pl.ANY)


def core_swap():
    return [(l * 16 + t, l * 16 + (t ^ 1)) for l in range(LEVELS) for t in range(16)]


def chip_swap():
    return [(l * 16 + t, l * 16 + (t + (1 if t % 2 else 15)) % 16) for l in range(LEVELS) for t in range(16)]


def level_swap(by):
    return [(l * 16 + t, (l ^ by) * 16 + t) for l in range(LEVELS) if l ^ by < LEVELS for t in range(16)]


def send(value, pairs):
    return lax.ppermute(value, ("level", "tile"), pairs)


def everyone(value):
    return lax.all_to_all(value, "level", 0, 0)


def on_first_core():
    return lax.rem(lax.axis_index("tile"), 2) == 0


def cut_kernel(state_hbm, hist_hbm, out_ref, *refs):
    lasts, (state, hist, tiles, turned, in_sem, out_sem) = refs[:LEVELS], refs[LEVELS:]
    loads = [pltpu.make_async_copy(state_hbm, state, in_sem.at[0])]
    loads += [pltpu.make_async_copy(hist_hbm.at[n], hist.at[n], in_sem.at[n + 1]) for n in range(3)]
    for load in loads:
        load.start()

    def turn(n, value):
        tiles[n] = value
        rows = [tiles[n, pl.ds(row, SPECIES, stride=ROWS), :] for row in range(ROWS)]
        return jnp.concatenate(rows, axis=0).T

    def put(n, chunk, half, value):
        start = n * WIDE
        out_ref[chunk, start + HALO + half * 128 : start + HALO + (half + 1) * 128, :] = value
        if half == 0:
            other = lax.rem(chunk + LEVELS - 1, LEVELS)
            out_ref[other, start + WIDE - HALO : start + WIDE, :] = value[:HALO]
        else:
            other = lax.rem(chunk + 1, LEVELS)
            out_ref[other, start : start + HALO, :] = value[128 - HALO :]

    def columns(chunk, half):
        return pl.ds(pl.multiple_of(chunk * CHUNK + half * 128, 128), 128)

    def last_body(i, _):
        for half in range(2):
            r = hist[2, :, columns(i, half)]
            at = pl.multiple_of(i * CHUNK + half * 128 + HALO, 8)
            turned[pl.ds(at, 128), :] = turn(3, (STEP * W0) * r)
        return 0

    def state_body(chunk, _):
        for half in range(2):
            put(0, chunk, half, turn(0, state[:, columns(chunk, half)]))
        return 0

    def hist_body(chunk, _):
        for half in range(2):
            p, q, r = (hist[n, :, columns(chunk, half)] for n in range(3))
            put(1, chunk, half, turn(1, STEP * (W0 * p + W1 * q + (W2 - 1.0) * r)))
            put(2, chunk, half, turn(2, STEP * (W0 * q + W1 * r)))
        return 0

    loads[0].wait()
    lax.fori_loop(0, LEVELS, state_body, 0)
    for load in loads[1:]:
        load.wait()
    lax.fori_loop(0, LEVELS, last_body, 0)
    turned[:HALO, :] = turned[NCOL : NCOL + HALO, :]
    turned[NCOL + HALO :, :] = turned[HALO : 2 * HALO, :]
    copies = []
    for by, last_ref in enumerate(lasts):
        base = pl.multiple_of(lax.bitwise_xor(lax.axis_index("level"), by) * CHUNK, 128)
        copies.append(pltpu.make_async_copy(turned.at[pl.ds(base, WIDE), :], last_ref, out_sem.at[by]))
        copies[-1].start()
    lax.fori_loop(0, LEVELS, hist_body, 0)
    for copy in copies:
        copy.wait()


def cut(state, hist):
    outs = pl.pallas_call(
        cut_kernel,
        out_shape=[pltpu.VMEM((LEVELS, 3 * WIDE, CELLS), f32)] + [jax.ShapeDtypeStruct((WIDE, CELLS), f32)] * LEVELS,
        in_specs=[hbm()] * 2,
        out_specs=[vmem()] + [hbm()] * LEVELS,
        scratch_shapes=[
            pltpu.VMEM((CELLS, NCOL), f32),
            pltpu.VMEM((3, CELLS, NCOL), f32),
            pltpu.VMEM((FIELDS, CELLS, 128), f32),
            pltpu.VMEM((NCOL + 2 * HALO, CELLS), f32),
            pltpu.SemaphoreType.DMA((4,)),
            pltpu.SemaphoreType.DMA((LEVELS,)),
        ],
        compiler_params=params(40),
        name="cut",
    )(state, hist)
    return outs[0], outs[1:]


def gather_kernel(*refs):
    parts, out_ref, sem = refs[:LEVELS], refs[LEVELS], refs[LEVELS + 1]
    copies = []
    for by, part in enumerate(parts):
        level = lax.bitwise_xor(lax.axis_index("level"), by)
        copies.append(pltpu.make_async_copy(part, out_ref.at[level], sem.at[by]))
        copies[-1].start()
    for copy in copies:
        copy.wait()


def gather(parts):
    return pl.pallas_call(
        gather_kernel,
        out_shape=pltpu.VMEM((LEVELS, WIDE, CELLS), f32),
        in_specs=[hbm()] * LEVELS,
        out_specs=vmem(),
        scratch_shapes=[pltpu.SemaphoreType.DMA((LEVELS,))],
        compiler_params=params(),
        name="gather",
    )(*parts)


def pack_edges(u_ref, inner_ref, outer_ref):
    lane = lax.broadcasted_iota(jnp.int32, (BAND, HALF), 1)
    first_core = on_first_core()
    for group in range(LEVELS // GROUP):
        at = slice(group * HALF, (group + 1) * HALF)
        for begin in range(0, WIDE, BAND):
            rows = slice(begin, begin + BAND)
            down = up = None
            for k in range(GROUP):
                here = (lane >= k * EDGE) & (lane < (k + 1) * EDGE)
                top = u_ref[group * GROUP + k, rows, :HALF]
                bottom = u_ref[group * GROUP + k, rows, HALF:]
                top = pltpu.roll(top, k * EDGE, 1) if k else top
                bottom = pltpu.roll(bottom, (k + 1) * EDGE, 1) if k < GROUP - 1 else bottom
                down = top if k == 0 else jnp.where(here, top, down)
                up = bottom if k == 0 else jnp.where(here, bottom, up)
            inner_ref[rows, at] = jnp.where(first_core, up, down)
            outer_ref[rows, at] = jnp.where(first_core, down, up)


def edges_kernel(fields_ref, inner_ref, outer_ref):
    pack_edges(fields_ref, inner_ref, outer_ref)


HALO_SHAPE = jax.ShapeDtypeStruct((WIDE, LEVELS * EDGE), f32)


def first_edges(fields):
    return pl.pallas_call(
        edges_kernel,
        out_shape=[HALO_SHAPE] * 2,
        in_specs=[vmem()],
        out_specs=[vmem()] * 2,
        compiler_params=params(),
        name="edges",
    )(fields)


def split(into, at, value, rows=slice(0, WIDE)):
    high_part = value.astype(bf16)
    width = value.shape[1]
    into[rows, at : at + width] = high_part
    into[rows, CELLS + at : CELLS + at + width] = (value - high_part.astype(f32)).astype(bf16)
    into[rows, 2 * CELLS + at : 2 * CELLS + at + width] = high_part


def inner_kernel(u_ref, main_ref, diff_ref, rate_ref, padded, stack):
    padded[:, :, :PAD, :] = jnp.zeros((2, 2, PAD, HALF), f32)
    padded[:, :, PAD + WIDE :, :] = jnp.zeros((2, 2, PAD, HALF), f32)
    for pair in range(LEVELS // 2):
        for k in range(2):
            for side in range(2):
                part = u_ref[2 * pair + k, :WIDE, side * HALF : (side + 1) * HALF]
                padded[k, side, PAD : PAD + WIDE, :] = part
                split(stack, side * HALF, part, slice(k * WIDE, (k + 1) * WIDE))
        products = dot(stack[...], main_ref[...])
        for k in range(2):
            for side in range(2):
                at = slice(side * HALF, (side + 1) * HALF)
                diff = diff_ref[0:1, at]
                for begin in range(0, WIDE, BAND):
                    moved = lambda by: padded[k, side, PAD + begin + by : PAD + begin + by + BAND, :]
                    rows = slice(k * WIDE + begin, k * WIDE + begin + BAND)
                    u = moved(0)
                    near = moved(-1) + moved(1)
                    far = moved(-2) + moved(2)
                    rate = products[rows, at] + diff * (16.0 * near - far)
                    rate = rate + jnp.tanh(products[rows, CELLS + side * HALF : CELLS + (side + 1) * HALF])
                    rate_ref[2 * pair + k, begin : begin + BAND, at] = rate - u * u * u * (1.0 / 3.0)


def inner_rates(step, u, weights):
    main, _, diff = weights
    return pl.pallas_call(
        inner_kernel,
        out_shape=pltpu.VMEM((LEVELS, WIDE, CELLS), f32),
        in_specs=[vmem()] * 3,
        out_specs=vmem(),
        scratch_shapes=[
            pltpu.VMEM((2, 2, WIDE + 2 * PAD, HALF), f32),
            pltpu.VMEM((2 * WIDE, 3 * CELLS), bf16),
        ],
        compiler_params=params(),
        name=f"inner_{step}",
    )(u, main, diff)


def step_kernel(step, n_in, n_out, u_ref, rate_ref, inner_ref, outer_ref, edge_ref, *refs):
    refs = list(refs)
    take = lambda n: [refs.pop(0) for _ in range(n)]
    fields_ref = take(1)[0] if step < 3 else None
    older = take(n_in)
    next_ref = take(1)[0]
    sends = take(2) if step < 3 else None
    newer = take(n_out)
    stack, edges = take(2)
    first_core = on_first_core()
    for group in range(LEVELS // GROUP):
        at = slice(group * HALF, (group + 1) * HALF)
        inner, outer = inner_ref[:, at], outer_ref[:, at]
        split(stack, 0, jnp.where(first_core, outer, inner))
        split(stack, HALF, jnp.where(first_core, inner, outer))
        edges[group] = dot(stack[...], edge_ref[...])
    lane = lax.broadcasted_iota(jnp.int32, (BAND, HALF), 1)
    for side in range(2):
        at = slice(side * HALF, (side + 1) * HALF)
        near_edge = lane >= HALF - EDGE if side else lane < EDGE
        for begin in range(0, WIDE, BAND):
            rows = slice(begin, begin + BAND)
            below = None
            for level in range(LEVELS):
                group, k = divmod(level, GROUP)
                turn = (HALF - EDGE - k * EDGE if side else HALF - k * EDGE) % HALF
                edge = edges[group, rows, at]
                edge = pltpu.roll(edge, turn, 1) if turn else edge
                scaled = STEP * (rate_ref[level, rows, at] + jnp.where(near_edge, edge, 0.0))
                value = u_ref[level, rows, at] + scaled
                next_ref[level, rows, at] = value if below is None else value + below
                below = W3 * scaled
                if n_in > 0:
                    below = below + older[0][level, rows, at]
                if step < 3:
                    start = (0 if step == 2 else (step + 1) * WIDE) + begin
                    below = below + fields_ref[level, start : start + BAND, at]
                for i, weight in zip(range(n_out), (W2 - 1.0, W1, W0)):
                    value = weight * scaled
                    if i + 1 < n_in:
                        value = value + older[i + 1][level, rows, at]
                    newer[i][level, rows, at] = value
    if step < 3:
        pack_edges(next_ref, *sends)


def one_step(step, u, rate, inner, outer, weights, fields, older, n_out):
    n_in = len(older)
    full = pltpu.VMEM((LEVELS, WIDE, CELLS), f32)
    operands = [u, rate, inner, outer, weights[1]] + ([fields] if step < 3 else []) + older
    outs = [full] + ([HALO_SHAPE] * 2 if step < 3 else []) + [full] * n_out
    outs = pl.pallas_call(
        functools.partial(step_kernel, step, n_in, n_out),
        out_shape=outs,
        in_specs=[vmem()] * len(operands),
        out_specs=[vmem()] * len(outs),
        scratch_shapes=[
            pltpu.VMEM((WIDE, 3 * CELLS), bf16),
            pltpu.VMEM((LEVELS // GROUP, WIDE, CELLS), f32),
        ],
        compiler_params=params(),
        name=f"step_{step}",
    )(*operands)
    if step < 3:
        return outs[0], outs[1], outs[2], list(outs[3:])
    return outs[0], None, None, []


def weights_kernel(lin_ref, coup_ref, diff_ref, main_ref, edge_ref, diff_out):
    exact = functools.partial(lax.dot_general, precision=lax.Precision.HIGHEST, preferred_element_type=f32)
    last = (((1,), (1,)), ((), ()))
    iota = lambda shape, dim: lax.broadcasted_iota(jnp.int32, shape, dim)
    pick = (iota((CELLS, SPECIES), 0) % SPECIES == iota((CELLS, SPECIES), 1)).astype(f32)
    source, target = iota((CELLS, CELLS), 0), iota((CELLS, CELLS), 1)
    same_row = source // SPECIES == target // SPECIES
    same_species = source % SPECIES == target % SPECIES
    diffusion = exact(diff_ref[...], pick, last)

    def tiled(matrix):
        return jnp.where(same_row, exact(exact(pick, matrix, last), pick, last), 0.0)

    def stencil(offset, middle):
        value = jnp.where(offset == 0, middle, 0.0)
        value = value + jnp.where((offset == 1) | (offset == -1), TAPS[1], 0.0)
        return value + jnp.where((offset == 2) | (offset == -2), TAPS[0], 0.0)

    def put(into, at, value):
        high_part = value.astype(bf16)
        into[:CELLS, at : at + CELLS] = high_part
        into[CELLS : 2 * CELLS, at : at + CELLS] = high_part
        into[2 * CELLS :, at : at + CELLS] = (value - high_part.astype(f32)).astype(bf16)

    offset = source // SPECIES - target // SPECIES
    spread = jnp.where(same_species, stencil(offset, 2.0 * TAPS[2]) * diffusion[0:1], 0.0)
    put(main_ref, 0, tiled(lin_ref[...]) + spread)
    put(main_ref, CELLS, tiled(coup_ref[...]))
    row_from = (source // SPECIES) % 2 + jnp.where(source < HALF, -2, ROWS)
    row_to = (target // SPECIES) % 2 + jnp.where(target < HALF, 0, ROWS - 2)
    alike = same_species & (source // EDGE == target // EDGE)
    put(edge_ref, 0, jnp.where(alike, stencil(row_from - row_to, 0.0) * diffusion[0:1], 0.0))
    diff_out[...] = diffusion * (1.0 / 12.0)


def make_weights(diffusion, linear_rates, coupling):
    return pl.pallas_call(
        weights_kernel,
        out_shape=[
            pltpu.VMEM((3 * CELLS, 2 * CELLS), bf16),
            pltpu.VMEM((3 * CELLS, CELLS), bf16),
            pltpu.VMEM((8, CELLS), f32),
        ],
        in_specs=[vmem()] * 3,
        out_specs=[vmem()] * 3,
        compiler_params=params(),
        name="weights",
    )(linear_rates, coupling, jnp.broadcast_to(diffusion[None], (8, SPECIES)))


def join_kernel(parts, out_ref, turn, whole, sem):
    copies = []
    for half in range(2):
        for slot in range(NCOL // 128):
            chunk, i = divmod(slot, CHUNK // 128)
            turn[slot] = parts[chunk, i * 128 : (i + 1) * 128, half * HALF : (half + 1) * HALF].T
            columns = slice(slot * 128, (slot + 1) * 128)
            for species in range(SPECIES):
                whole[half, species, :, columns] = turn[slot, pl.ds(species, ROWS // 2, stride=SPECIES), :]
        target = out_ref.at[:, half * (ROWS // 2) : (half + 1) * (ROWS // 2), :]
        copies.append(pltpu.make_async_copy(whole.at[half], target, sem.at[half]))
        copies[-1].start()
    for copy in copies:
        copy.wait()


def join(parts):
    return pl.pallas_call(
        join_kernel,
        out_shape=jax.ShapeDtypeStruct((SPECIES, ROWS, NCOL), f32),
        in_specs=[vmem()],
        out_specs=hbm(),
        scratch_shapes=[
            pltpu.VMEM((NCOL // 128, HALF, 128), f32),
            pltpu.VMEM((2, SPECIES, ROWS // 2, NCOL), f32),
            pltpu.SemaphoreType.DMA((2,)),
        ],
        compiler_params=params(),
        name="join",
    )(parts)


def after(value, *earlier):
    return lax.optimization_barrier((value, *earlier))[0]


WAVES = ((1, 3), (4, 2, 5), (6, 7))


def local(level_state, history, diffusion, linear_rates, coupling):
    state = level_state.reshape(CELLS, NCOL)
    hist = history.reshape(3, CELLS, NCOL)
    weights = make_weights(diffusion, linear_rates, coupling)
    first, lasts = cut(state, hist)
    fields = everyone(first)
    u = fields
    inner, outer = first_edges(fields)
    older = []
    got = {0: lasts[0]}
    edge = inner
    for step, n_out in enumerate((3, 2, 1, 0)):
        outer = send(outer, chip_swap())
        inner = send(inner, core_swap())
        earlier = list(got.values()) if step else [fields, edge]
        if step < 3:
            for by in WAVES[step]:
                got[by] = send(after(lasts[by], *earlier), level_swap(by))
        rate = inner_rates(step, after(u, *earlier) if step else u, weights)
        if step == 2:
            fields = gather([got[by] for by in range(LEVELS)])
        u, inner, outer, older = one_step(step, u, rate, inner, outer, weights, fields, older, n_out)
    return join(everyone(u[:, HALO : HALO + CHUNK, :]))[None]


def solution(mesh):
    placed = (P("level", None, "tile", None), P("level", None, None, "tile", None), P(), P(), P())
    return jax.shard_map(
        local, mesh=mesh, in_specs=placed, out_specs=P("level", None, "tile", None), check_vma=False
    )
```

```python
import functools

import jax
import jax.numpy as jnp
from jax import lax
from jax.experimental import pallas as pl
from jax.experimental.pallas import tpu as pltpu
from jax.sharding import PartitionSpec as P

SPECIES = 16
ROWS = 16
CELLS = SPECIES * ROWS
HALF = CELLS // 2
NCOL = 2048
LEVELS = 8
CHUNK = NCOL // LEVELS
HALO = 8
WIDE = CHUNK + 2 * HALO
EDGE = 2 * SPECIES
STEP = 0.4
W0, W1, W2, W3 = (1.0 / 24.0, -5.0 / 24.0, 19.0 / 24.0, 9.0 / 24.0)
TAPS = (-1.0 / 12.0, 16.0 / 12.0, -30.0 / 12.0, 16.0 / 12.0, -1.0 / 12.0)
PAD = 8
FIELDS = 4
GROUP = HALF // EDGE
BAND = WIDE // 2

f32 = jnp.float32
bf16 = jnp.bfloat16
dot = functools.partial(jnp.dot, preferred_element_type=f32)


def params(mib=24, **kw):
    return pltpu.CompilerParams(vmem_limit_bytes=mib * 1024 * 1024, **kw)


def vmem():
    return pl.BlockSpec(memory_space=pltpu.VMEM)


def hbm():
    return pl.BlockSpec(memory_space=pl.ANY)


def core_swap():
    return [(l * 16 + t, l * 16 + (t ^ 1)) for l in range(LEVELS) for t in range(16)]


def chip_swap():
    return [(l * 16 + t, l * 16 + (t + (1 if t % 2 else 15)) % 16) for l in range(LEVELS) for t in range(16)]


def level_swap(by):
    return [(l * 16 + t, (l ^ by) * 16 + t) for l in range(LEVELS) if l ^ by < LEVELS for t in range(16)]


def send(value, pairs):
    return lax.ppermute(value, ("level", "tile"), pairs)


def everyone(value):
    return lax.all_to_all(value, "level", 0, 0)


def on_first_core():
    return lax.rem(lax.axis_index("tile"), 2) == 0


def cut_kernel(state_hbm, hist_hbm, out_ref, *refs):
    lasts, (state, hist, tiles, turned, in_sem, out_sem) = refs[:LEVELS], refs[LEVELS:]
    loads = [pltpu.make_async_copy(state_hbm, state, in_sem.at[0])]
    loads += [pltpu.make_async_copy(hist_hbm.at[n], hist.at[n], in_sem.at[n + 1]) for n in range(3)]
    for load in loads:
        load.start()

    def turn(n, value):
        tiles[n] = value
        rows = [tiles[n, pl.ds(row, SPECIES, stride=ROWS), :] for row in range(ROWS)]
        return jnp.concatenate(rows, axis=0).T

    def put(n, chunk, half, value):
        start = n * WIDE
        out_ref[chunk, start + HALO + half * 128 : start + HALO + (half + 1) * 128, :] = value
        if half == 0:
            other = lax.rem(chunk + LEVELS - 1, LEVELS)
            out_ref[other, start + WIDE - HALO : start + WIDE, :] = value[:HALO]
        else:
            other = lax.rem(chunk + 1, LEVELS)
            out_ref[other, start : start + HALO, :] = value[128 - HALO :]

    def columns(chunk, half):
        return pl.ds(pl.multiple_of(chunk * CHUNK + half * 128, 128), 128)

    def last_body(i, _):
        for half in range(2):
            r = hist[2, :, columns(i, half)]
            at = pl.multiple_of(i * CHUNK + half * 128 + HALO, 8)
            turned[pl.ds(at, 128), :] = turn(3, (STEP * W0) * r)
        return 0

    def state_body(chunk, _):
        for half in range(2):
            put(0, chunk, half, turn(0, state[:, columns(chunk, half)]))
        return 0

    def hist_body(chunk, _):
        for half in range(2):
            p, q, r = (hist[n, :, columns(chunk, half)] for n in range(3))
            put(1, chunk, half, turn(1, STEP * (W0 * p + W1 * q + (W2 - 1.0) * r)))
            put(2, chunk, half, turn(2, STEP * (W0 * q + W1 * r)))
        return 0

    loads[0].wait()
    lax.fori_loop(0, LEVELS, state_body, 0)
    for load in loads[1:]:
        load.wait()
    lax.fori_loop(0, LEVELS, last_body, 0)
    turned[:HALO, :] = turned[NCOL : NCOL + HALO, :]
    turned[NCOL + HALO :, :] = turned[HALO : 2 * HALO, :]
    copies = []
    for by, last_ref in enumerate(lasts):
        base = pl.multiple_of(lax.bitwise_xor(lax.axis_index("level"), by) * CHUNK, 128)
        copies.append(pltpu.make_async_copy(turned.at[pl.ds(base, WIDE), :], last_ref, out_sem.at[by]))
        copies[-1].start()
    lax.fori_loop(0, LEVELS, hist_body, 0)
    for copy in copies:
        copy.wait()


def cut(state, hist):
    outs = pl.pallas_call(
        cut_kernel,
        out_shape=[pltpu.VMEM((LEVELS, 3 * WIDE, CELLS), f32)] + [jax.ShapeDtypeStruct((WIDE, CELLS), f32)] * LEVELS,
        in_specs=[hbm()] * 2,
        out_specs=[vmem()] + [hbm()] * LEVELS,
        scratch_shapes=[
            pltpu.VMEM((CELLS, NCOL), f32),
            pltpu.VMEM((3, CELLS, NCOL), f32),
            pltpu.VMEM((FIELDS, CELLS, 128), f32),
            pltpu.VMEM((NCOL + 2 * HALO, CELLS), f32),
            pltpu.SemaphoreType.DMA((4,)),
            pltpu.SemaphoreType.DMA((LEVELS,)),
        ],
        compiler_params=params(54),
        name="cut",
    )(state, hist)
    return outs[0], outs[1:]


def gather_kernel(*refs):
    parts, out_ref, sem = refs[:LEVELS], refs[LEVELS], refs[LEVELS + 1]
    copies = []
    for by, part in enumerate(parts):
        level = lax.bitwise_xor(lax.axis_index("level"), by)
        copies.append(pltpu.make_async_copy(part, out_ref.at[level], sem.at[by]))
        copies[-1].start()
    for copy in copies:
        copy.wait()


def gather(parts):
    return pl.pallas_call(
        gather_kernel,
        out_shape=pltpu.VMEM((LEVELS, WIDE, CELLS), f32),
        in_specs=[hbm()] * LEVELS,
        out_specs=vmem(),
        scratch_shapes=[pltpu.SemaphoreType.DMA((LEVELS,))],
        compiler_params=params(),
        name="gather",
    )(*parts)


def pack_edges(u_ref, inner_ref, outer_ref):
    lane = lax.broadcasted_iota(jnp.int32, (BAND, HALF), 1)
    first_core = on_first_core()
    for group in range(LEVELS // GROUP):
        at = slice(group * HALF, (group + 1) * HALF)
        for begin in range(0, WIDE, BAND):
            rows = slice(begin, begin + BAND)
            down = up = None
            for k in range(GROUP):
                here = (lane >= k * EDGE) & (lane < (k + 1) * EDGE)
                top = u_ref[group * GROUP + k, rows, :HALF]
                bottom = u_ref[group * GROUP + k, rows, HALF:]
                top = pltpu.roll(top, k * EDGE, 1) if k else top
                bottom = pltpu.roll(bottom, (k + 1) * EDGE, 1) if k < GROUP - 1 else bottom
                down = top if k == 0 else jnp.where(here, top, down)
                up = bottom if k == 0 else jnp.where(here, bottom, up)
            inner_ref[rows, at] = jnp.where(first_core, up, down)
            outer_ref[rows, at] = jnp.where(first_core, down, up)


def edges_kernel(fields_ref, inner_ref, outer_ref):
    pack_edges(fields_ref, inner_ref, outer_ref)


HALO_SHAPE = jax.ShapeDtypeStruct((WIDE, LEVELS * EDGE), f32)


def first_edges(fields):
    return pl.pallas_call(
        edges_kernel,
        out_shape=[HALO_SHAPE] * 2,
        in_specs=[vmem()],
        out_specs=[vmem()] * 2,
        compiler_params=params(),
        name="edges",
    )(fields)


def split(into, at, value, rows=slice(0, WIDE)):
    high_part = value.astype(bf16)
    width = value.shape[1]
    into[rows, at : at + width] = high_part
    into[rows, CELLS + at : CELLS + at + width] = (value - high_part.astype(f32)).astype(bf16)
    into[rows, 2 * CELLS + at : 2 * CELLS + at + width] = high_part


def inner_kernel(u_ref, main_ref, diff_ref, rate_ref, padded, stack):
    padded[:, :, :PAD, :] = jnp.zeros((2, 2, PAD, HALF), f32)
    padded[:, :, PAD + WIDE :, :] = jnp.zeros((2, 2, PAD, HALF), f32)
    for pair in range(LEVELS // 2):
        for k in range(2):
            for side in range(2):
                part = u_ref[2 * pair + k, :WIDE, side * HALF : (side + 1) * HALF]
                padded[k, side, PAD : PAD + WIDE, :] = part
                split(stack, side * HALF, part, slice(k * WIDE, (k + 1) * WIDE))
        products = dot(stack[...], main_ref[...])
        for k in range(2):
            for side in range(2):
                at = slice(side * HALF, (side + 1) * HALF)
                diff = diff_ref[0:1, at]
                for begin in range(0, WIDE, BAND):
                    moved = lambda by: padded[k, side, PAD + begin + by : PAD + begin + by + BAND, :]
                    rows = slice(k * WIDE + begin, k * WIDE + begin + BAND)
                    u = moved(0)
                    near = moved(-1) + moved(1)
                    far = moved(-2) + moved(2)
                    rate = products[rows, at] + diff * (16.0 * near - far)
                    rate = rate + jnp.tanh(products[rows, CELLS + side * HALF : CELLS + (side + 1) * HALF])
                    rate_ref[2 * pair + k, begin : begin + BAND, at] = rate - u * u * u * (1.0 / 3.0)


def inner_rates(step, u, weights):
    main, _, diff = weights
    return pl.pallas_call(
        inner_kernel,
        out_shape=pltpu.VMEM((LEVELS, WIDE, CELLS), f32),
        in_specs=[vmem()] * 3,
        out_specs=vmem(),
        scratch_shapes=[
            pltpu.VMEM((2, 2, WIDE + 2 * PAD, HALF), f32),
            pltpu.VMEM((2 * WIDE, 3 * CELLS), bf16),
        ],
        compiler_params=params(),
        name=f"inner_{step}",
    )(u, main, diff)


def step_kernel(step, n_in, n_out, u_ref, rate_ref, inner_ref, outer_ref, edge_ref, *refs):
    refs = list(refs)
    take = lambda n: [refs.pop(0) for _ in range(n)]
    fields_ref = take(1)[0] if step < 3 else None
    older = take(n_in)
    next_ref = take(1)[0]
    sends = take(2) if step < 3 else None
    newer = take(n_out)
    stack, edges = take(2)
    first_core = on_first_core()
    for group in range(LEVELS // GROUP):
        at = slice(group * HALF, (group + 1) * HALF)
        inner, outer = inner_ref[:, at], outer_ref[:, at]
        split(stack, 0, jnp.where(first_core, outer, inner))
        split(stack, HALF, jnp.where(first_core, inner, outer))
        edges[group] = dot(stack[...], edge_ref[...])
    lane = lax.broadcasted_iota(jnp.int32, (BAND, HALF), 1)
    for side in range(2):
        at = slice(side * HALF, (side + 1) * HALF)
        near_edge = lane >= HALF - EDGE if side else lane < EDGE
        for begin in range(0, WIDE, BAND):
            rows = slice(begin, begin + BAND)
            below = None
            for level in range(LEVELS):
                group, k = divmod(level, GROUP)
                turn = (HALF - EDGE - k * EDGE if side else HALF - k * EDGE) % HALF
                edge = edges[group, rows, at]
                edge = pltpu.roll(edge, turn, 1) if turn else edge
                scaled = STEP * (rate_ref[level, rows, at] + jnp.where(near_edge, edge, 0.0))
                value = u_ref[level, rows, at] + scaled
                next_ref[level, rows, at] = value if below is None else value + below
                below = W3 * scaled
                if n_in > 0:
                    below = below + older[0][level, rows, at]
                if step < 3:
                    start = (0 if step == 2 else (step + 1) * WIDE) + begin
                    below = below + fields_ref[level, start : start + BAND, at]
                for i, weight in zip(range(n_out), (W2 - 1.0, W1, W0)):
                    value = weight * scaled
                    if i + 1 < n_in:
                        value = value + older[i + 1][level, rows, at]
                    newer[i][level, rows, at] = value
    if step < 3:
        pack_edges(next_ref, *sends)


def one_step(step, u, rate, inner, outer, weights, fields, older, n_out):
    n_in = len(older)
    full = pltpu.VMEM((LEVELS, WIDE, CELLS), f32)
    operands = [u, rate, inner, outer, weights[1]] + ([fields] if step < 3 else []) + older
    outs = [full] + ([HALO_SHAPE] * 2 if step < 3 else []) + [full] * n_out
    outs = pl.pallas_call(
        functools.partial(step_kernel, step, n_in, n_out),
        out_shape=outs,
        in_specs=[vmem()] * len(operands),
        out_specs=[vmem()] * len(outs),
        scratch_shapes=[
            pltpu.VMEM((WIDE, 3 * CELLS), bf16),
            pltpu.VMEM((LEVELS // GROUP, WIDE, CELLS), f32),
        ],
        compiler_params=params(),
        name=f"step_{step}",
    )(*operands)
    if step < 3:
        return outs[0], outs[1], outs[2], list(outs[3:])
    return outs[0], None, None, []


def weights_kernel(lin_ref, coup_ref, diff_ref, main_ref, edge_ref, diff_out):
    exact = functools.partial(lax.dot_general, precision=lax.Precision.HIGHEST, preferred_element_type=f32)
    last = (((1,), (1,)), ((), ()))
    iota = lambda shape, dim: lax.broadcasted_iota(jnp.int32, shape, dim)
    pick = (iota((CELLS, SPECIES), 0) % SPECIES == iota((CELLS, SPECIES), 1)).astype(f32)
    source, target = iota((CELLS, CELLS), 0), iota((CELLS, CELLS), 1)
    same_row = source // SPECIES == target // SPECIES
    same_species = source % SPECIES == target % SPECIES
    diffusion = exact(diff_ref[...], pick, last)

    def tiled(matrix):
        return jnp.where(same_row, exact(exact(pick, matrix, last), pick, last), 0.0)

    def stencil(offset, middle):
        value = jnp.where(offset == 0, middle, 0.0)
        value = value + jnp.where((offset == 1) | (offset == -1), TAPS[1], 0.0)
        return value + jnp.where((offset == 2) | (offset == -2), TAPS[0], 0.0)

    def put(into, at, value):
        high_part = value.astype(bf16)
        into[:CELLS, at : at + CELLS] = high_part
        into[CELLS : 2 * CELLS, at : at + CELLS] = high_part
        into[2 * CELLS :, at : at + CELLS] = (value - high_part.astype(f32)).astype(bf16)

    offset = source // SPECIES - target // SPECIES
    spread = jnp.where(same_species, stencil(offset, 2.0 * TAPS[2]) * diffusion[0:1], 0.0)
    put(main_ref, 0, tiled(lin_ref[...]) + spread)
    put(main_ref, CELLS, tiled(coup_ref[...]))
    row_from = (source // SPECIES) % 2 + jnp.where(source < HALF, -2, ROWS)
    row_to = (target // SPECIES) % 2 + jnp.where(target < HALF, 0, ROWS - 2)
    alike = same_species & (source // EDGE == target // EDGE)
    put(edge_ref, 0, jnp.where(alike, stencil(row_from - row_to, 0.0) * diffusion[0:1], 0.0))
    diff_out[...] = diffusion * (1.0 / 12.0)


def make_weights(diffusion, linear_rates, coupling):
    return pl.pallas_call(
        weights_kernel,
        out_shape=[
            pltpu.VMEM((3 * CELLS, 2 * CELLS), bf16),
            pltpu.VMEM((3 * CELLS, CELLS), bf16),
            pltpu.VMEM((8, CELLS), f32),
        ],
        in_specs=[vmem()] * 3,
        out_specs=[vmem()] * 3,
        compiler_params=params(),
        name="weights",
    )(linear_rates, coupling, jnp.broadcast_to(diffusion[None], (8, SPECIES)))


def join_kernel(parts, out_ref, turn, whole, sem):
    copies = []
    for half in range(2):
        for slot in range(NCOL // 128):
            chunk, i = divmod(slot, CHUNK // 128)
            turn[slot] = parts[chunk, i * 128 : (i + 1) * 128, half * HALF : (half + 1) * HALF].T
            columns = slice(slot * 128, (slot + 1) * 128)
            for species in range(SPECIES):
                whole[half, species, :, columns] = turn[slot, pl.ds(species, ROWS // 2, stride=SPECIES), :]
        target = out_ref.at[:, half * (ROWS // 2) : (half + 1) * (ROWS // 2), :]
        copies.append(pltpu.make_async_copy(whole.at[half], target, sem.at[half]))
        copies[-1].start()
    for copy in copies:
        copy.wait()


def join(parts):
    return pl.pallas_call(
        join_kernel,
        out_shape=jax.ShapeDtypeStruct((SPECIES, ROWS, NCOL), f32),
        in_specs=[vmem()],
        out_specs=hbm(),
        scratch_shapes=[
            pltpu.VMEM((NCOL // 128, HALF, 128), f32),
            pltpu.VMEM((2, SPECIES, ROWS // 2, NCOL), f32),
            pltpu.SemaphoreType.DMA((2,)),
        ],
        compiler_params=params(),
        name="join",
    )(parts)


def after(value, *earlier):
    return lax.optimization_barrier((value, *earlier))[0]


WAVES = ((1, 3), (4, 2, 5), (6, 7))


def local(level_state, history, diffusion, linear_rates, coupling):
    state = level_state.reshape(CELLS, NCOL)
    hist = history.reshape(3, CELLS, NCOL)
    weights = make_weights(diffusion, linear_rates, coupling)
    first, lasts = cut(state, hist)
    fields = everyone(first)
    u = fields
    inner, outer = first_edges(fields)
    older = []
    got = {0: lasts[0]}
    edge = inner
    for step, n_out in enumerate((3, 2, 1, 0)):
        outer = send(outer, chip_swap())
        inner = send(inner, core_swap())
        earlier = list(got.values()) if step else [fields, edge]
        if step < 3:
            for by in WAVES[step]:
                got[by] = send(after(lasts[by], *earlier), level_swap(by))
        rate = inner_rates(step, after(u, *earlier) if step else u, weights)
        if step == 2:
            fields = gather([got[by] for by in range(LEVELS)])
        u, inner, outer, older = one_step(step, u, rate, inner, outer, weights, fields, older, n_out)
    return join(everyone(u[:, HALO : HALO + CHUNK, :]))[None]


def solution(mesh):
    placed = (P("level", None, "tile", None), P("level", None, None, "tile", None), P(), P(), P())
    return jax.shard_map(
        local, mesh=mesh, in_specs=placed, out_specs=P("level", None, "tile", None), check_vma=False
    )
```

```python
import functools

import jax
import jax.numpy as jnp
from jax import lax
from jax.experimental import pallas as pl
from jax.experimental.pallas import tpu as pltpu
from jax.sharding import PartitionSpec as P

SPECIES = 16
ROWS = 16
CELLS = SPECIES * ROWS
HALF = CELLS // 2
NCOL = 2048
LEVELS = 8
CHUNK = NCOL // LEVELS
HALO = 8
WIDE = CHUNK + 2 * HALO
EDGE = 2 * SPECIES
STEP = 0.4
W0, W1, W2, W3 = (1.0 / 24.0, -5.0 / 24.0, 19.0 / 24.0, 9.0 / 24.0)
TAPS = (-1.0 / 12.0, 16.0 / 12.0, -30.0 / 12.0, 16.0 / 12.0, -1.0 / 12.0)
PAD = 8
FIELDS = 4
GROUP = HALF // EDGE
BAND = WIDE // 2

f32 = jnp.float32
bf16 = jnp.bfloat16
dot = functools.partial(jnp.dot, preferred_element_type=f32)


def params(mib=24, **kw):
    return pltpu.CompilerParams(vmem_limit_bytes=mib * 1024 * 1024, **kw)


def vmem():
    return pl.BlockSpec(memory_space=pltpu.VMEM)


def hbm():
    return pl.BlockSpec(memory_space=pl.ANY)


def core_swap():
    return [(l * 16 + t, l * 16 + (t ^ 1)) for l in range(LEVELS) for t in range(16)]


def chip_swap():
    return [(l * 16 + t, l * 16 + (t + (1 if t % 2 else 15)) % 16) for l in range(LEVELS) for t in range(16)]


def level_swap(by):
    return [(l * 16 + t, (l ^ by) * 16 + t) for l in range(LEVELS) if l ^ by < LEVELS for t in range(16)]


def send(value, pairs):
    return lax.ppermute(value, ("level", "tile"), pairs)


def everyone(value):
    return lax.all_to_all(value, "level", 0, 0)


def on_first_core():
    return lax.rem(lax.axis_index("tile"), 2) == 0


def cut_kernel(state_hbm, hist_hbm, out_ref, *refs):
    lasts, (state, hist, tiles, turned, in_sem, out_sem) = refs[:LEVELS], refs[LEVELS:]
    loads = [pltpu.make_async_copy(state_hbm, state, in_sem.at[0])]
    loads += [pltpu.make_async_copy(hist_hbm.at[n], hist.at[n], in_sem.at[n + 1]) for n in range(3)]
    for load in loads:
        load.start()

    def turn(n, value):
        tiles[n] = value
        rows = [tiles[n, pl.ds(row, SPECIES, stride=ROWS), :] for row in range(ROWS)]
        return jnp.concatenate(rows, axis=0).T

    def put(n, chunk, half, value):
        start = n * WIDE
        out_ref[chunk, start + HALO + half * 128 : start + HALO + (half + 1) * 128, :] = value
        if half == 0:
            other = lax.rem(chunk + LEVELS - 1, LEVELS)
            out_ref[other, start + WIDE - HALO : start + WIDE, :] = value[:HALO]
        else:
            other = lax.rem(chunk + 1, LEVELS)
            out_ref[other, start : start + HALO, :] = value[128 - HALO :]

    def columns(chunk, half):
        return pl.ds(pl.multiple_of(chunk * CHUNK + half * 128, 128), 128)

    def last_body(i, _):
        for half in range(2):
            r = hist[2, :, columns(i, half)]
            at = pl.multiple_of(i * CHUNK + half * 128 + HALO, 8)
            turned[pl.ds(at, 128), :] = turn(3, (STEP * W0) * r)
        return 0

    def state_body(chunk, _):
        for half in range(2):
            put(0, chunk, half, turn(0, state[:, columns(chunk, half)]))
        return 0

    def hist_body(chunk, _):
        for half in range(2):
            p, q, r = (hist[n, :, columns(chunk, half)] for n in range(3))
            put(1, chunk, half, turn(1, STEP * (W0 * p + W1 * q + (W2 - 1.0) * r)))
            put(2, chunk, half, turn(2, STEP * (W0 * q + W1 * r)))
        return 0

    loads[0].wait()
    lax.fori_loop(0, LEVELS, state_body, 0)
    for load in loads[1:]:
        load.wait()
    lax.fori_loop(0, LEVELS, last_body, 0)
    turned[:HALO, :] = turned[NCOL : NCOL + HALO, :]
    turned[NCOL + HALO :, :] = turned[HALO : 2 * HALO, :]
    copies = []
    for by, last_ref in enumerate(lasts):
        base = pl.multiple_of(lax.bitwise_xor(lax.axis_index("level"), by) * CHUNK, 128)
        copies.append(pltpu.make_async_copy(turned.at[pl.ds(base, WIDE), :], last_ref, out_sem.at[by]))
        copies[-1].start()
    lax.fori_loop(0, LEVELS, hist_body, 0)
    for copy in copies:
        copy.wait()


def cut(state, hist):
    outs = pl.pallas_call(
        cut_kernel,
        out_shape=[pltpu.VMEM((LEVELS, 3 * WIDE, CELLS), f32)] + [jax.ShapeDtypeStruct((WIDE, CELLS), f32)] * LEVELS,
        in_specs=[hbm()] * 2,
        out_specs=[vmem()] + [hbm()] * LEVELS,
        scratch_shapes=[
            pltpu.VMEM((CELLS, NCOL), f32),
            pltpu.VMEM((3, CELLS, NCOL), f32),
            pltpu.VMEM((FIELDS, CELLS, 128), f32),
            pltpu.VMEM((NCOL + 2 * HALO, CELLS), f32),
            pltpu.SemaphoreType.DMA((4,)),
            pltpu.SemaphoreType.DMA((LEVELS,)),
        ],
        compiler_params=params(54),
        name="cut",
    )(state, hist)
    return outs[0], outs[1:]


def gather_kernel(*refs):
    parts, out_ref, sem = refs[:LEVELS], refs[LEVELS], refs[LEVELS + 1]
    copies = []
    for by, part in enumerate(parts):
        level = lax.bitwise_xor(lax.axis_index("level"), by)
        copies.append(pltpu.make_async_copy(part, out_ref.at[level], sem.at[by]))
        copies[-1].start()
    for copy in copies:
        copy.wait()


def gather(parts):
    return pl.pallas_call(
        gather_kernel,
        out_shape=pltpu.VMEM((LEVELS, WIDE, CELLS), f32),
        in_specs=[hbm()] * LEVELS,
        out_specs=vmem(),
        scratch_shapes=[pltpu.SemaphoreType.DMA((LEVELS,))],
        compiler_params=params(),
        name="gather",
    )(*parts)


def pack_edges(u_ref, inner_ref, outer_ref):
    lane = lax.broadcasted_iota(jnp.int32, (BAND, HALF), 1)
    first_core = on_first_core()
    for group in range(LEVELS // GROUP):
        at = slice(group * HALF, (group + 1) * HALF)
        for begin in range(0, WIDE, BAND):
            rows = slice(begin, begin + BAND)
            down = up = None
            for k in range(GROUP):
                here = (lane >= k * EDGE) & (lane < (k + 1) * EDGE)
                top = u_ref[group * GROUP + k, rows, :HALF]
                bottom = u_ref[group * GROUP + k, rows, HALF:]
                top = pltpu.roll(top, k * EDGE, 1) if k else top
                bottom = pltpu.roll(bottom, (k + 1) * EDGE, 1) if k < GROUP - 1 else bottom
                down = top if k == 0 else jnp.where(here, top, down)
                up = bottom if k == 0 else jnp.where(here, bottom, up)
            inner_ref[rows, at] = jnp.where(first_core, up, down)
            outer_ref[rows, at] = jnp.where(first_core, down, up)


def edges_kernel(fields_ref, inner_ref, outer_ref):
    pack_edges(fields_ref, inner_ref, outer_ref)


HALO_SHAPE = jax.ShapeDtypeStruct((WIDE, LEVELS * EDGE), f32)


def first_edges(fields):
    return pl.pallas_call(
        edges_kernel,
        out_shape=[HALO_SHAPE] * 2,
        in_specs=[vmem()],
        out_specs=[vmem()] * 2,
        compiler_params=params(),
        name="edges",
    )(fields)


def split(into, at, value, rows=slice(0, WIDE)):
    high_part = value.astype(bf16)
    width = value.shape[1]
    into[rows, at : at + width] = high_part
    into[rows, CELLS + at : CELLS + at + width] = (value - high_part.astype(f32)).astype(bf16)
    into[rows, 2 * CELLS + at : 2 * CELLS + at + width] = high_part


def inner_kernel(u_ref, main_ref, diff_ref, rate_ref, padded, stack):
    padded[:, :, :PAD, :] = jnp.zeros((2, 2, PAD, HALF), f32)
    padded[:, :, PAD + WIDE :, :] = jnp.zeros((2, 2, PAD, HALF), f32)
    for pair in range(LEVELS // 2):
        for k in range(2):
            for side in range(2):
                part = u_ref[2 * pair + k, :WIDE, side * HALF : (side + 1) * HALF]
                padded[k, side, PAD : PAD + WIDE, :] = part
                split(stack, side * HALF, part, slice(k * WIDE, (k + 1) * WIDE))
        products = dot(stack[...], main_ref[...])
        for k in range(2):
            for side in range(2):
                at = slice(side * HALF, (side + 1) * HALF)
                diff = diff_ref[0:1, at]
                for begin in range(0, WIDE, BAND):
                    moved = lambda by: padded[k, side, PAD + begin + by : PAD + begin + by + BAND, :]
                    rows = slice(k * WIDE + begin, k * WIDE + begin + BAND)
                    u = moved(0)
                    near = moved(-1) + moved(1)
                    far = moved(-2) + moved(2)
                    rate = products[rows, at] + diff * (16.0 * near - far)
                    rate = rate + jnp.tanh(products[rows, CELLS + side * HALF : CELLS + (side + 1) * HALF])
                    rate_ref[2 * pair + k, begin : begin + BAND, at] = rate - u * u * u * (1.0 / 3.0)


def inner_rates(step, u, weights):
    main, _, diff = weights
    return pl.pallas_call(
        inner_kernel,
        out_shape=pltpu.VMEM((LEVELS, WIDE, CELLS), f32),
        in_specs=[vmem()] * 3,
        out_specs=vmem(),
        scratch_shapes=[
            pltpu.VMEM((2, 2, WIDE + 2 * PAD, HALF), f32),
            pltpu.VMEM((2 * WIDE, 3 * CELLS), bf16),
        ],
        compiler_params=params(),
        name=f"inner_{step}",
    )(u, main, diff)


def step_kernel(step, n_in, n_out, u_ref, rate_ref, inner_ref, outer_ref, edge_ref, *refs):
    refs = list(refs)
    take = lambda n: [refs.pop(0) for _ in range(n)]
    fields_ref = take(1)[0] if step < 3 else None
    older = take(n_in)
    next_ref = take(1)[0]
    sends = take(2) if step < 3 else None
    newer = take(n_out)
    stack, edges = take(2)
    first_core = on_first_core()
    for group in range(LEVELS // GROUP):
        at = slice(group * HALF, (group + 1) * HALF)
        inner, outer = inner_ref[:, at], outer_ref[:, at]
        split(stack, 0, jnp.where(first_core, outer, inner))
        split(stack, HALF, jnp.where(first_core, inner, outer))
        edges[group] = dot(stack[...], edge_ref[...])
    lane = lax.broadcasted_iota(jnp.int32, (BAND, HALF), 1)
    for side in range(2):
        at = slice(side * HALF, (side + 1) * HALF)
        near_edge = lane >= HALF - EDGE if side else lane < EDGE
        for begin in range(0, WIDE, BAND):
            rows = slice(begin, begin + BAND)
            below = None
            for level in range(LEVELS):
                group, k = divmod(level, GROUP)
                turn = (HALF - EDGE - k * EDGE if side else HALF - k * EDGE) % HALF
                edge = edges[group, rows, at]
                edge = pltpu.roll(edge, turn, 1) if turn else edge
                scaled = STEP * (rate_ref[level, rows, at] + jnp.where(near_edge, edge, 0.0))
                value = u_ref[level, rows, at] + scaled
                value = value if below is None else value + below
                if step < 3:
                    next_ref[level, rows, at] = value
                else:
                    low, high = max(begin, HALO), min(begin + BAND, HALO + CHUNK)
                    next_ref[level, low - HALO : high - HALO, at] = value[low - begin : high - begin]
                below = W3 * scaled
                if n_in > 0:
                    below = below + older[0][level, rows, at]
                if step < 3:
                    start = (0 if step == 2 else (step + 1) * WIDE) + begin
                    below = below + fields_ref[level, start : start + BAND, at]
                for i, weight in zip(range(n_out), (W2 - 1.0, W1, W0)):
                    value = weight * scaled
                    if i + 1 < n_in:
                        value = value + older[i + 1][level, rows, at]
                    newer[i][level, rows, at] = value
    if step < 3:
        pack_edges(next_ref, *sends)


def one_step(step, u, rate, inner, outer, weights, fields, older, n_out):
    n_in = len(older)
    full = pltpu.VMEM((LEVELS, WIDE, CELLS), f32)
    operands = [u, rate, inner, outer, weights[1]] + ([fields] if step < 3 else []) + older
    state = full if step < 3 else pltpu.VMEM((LEVELS, CHUNK, CELLS), f32)
    outs = [state] + ([HALO_SHAPE] * 2 if step < 3 else []) + [full] * n_out
    outs = pl.pallas_call(
        functools.partial(step_kernel, step, n_in, n_out),
        out_shape=outs,
        in_specs=[vmem()] * len(operands),
        out_specs=[vmem()] * len(outs),
        scratch_shapes=[
            pltpu.VMEM((WIDE, 3 * CELLS), bf16),
            pltpu.VMEM((LEVELS // GROUP, WIDE, CELLS), f32),
        ],
        compiler_params=params(),
        name=f"step_{step}",
    )(*operands)
    if step < 3:
        return outs[0], outs[1], outs[2], list(outs[3:])
    return outs[0], None, None, []


def weights_kernel(lin_ref, coup_ref, diff_ref, main_ref, edge_ref, diff_out):
    exact = functools.partial(lax.dot_general, precision=lax.Precision.HIGHEST, preferred_element_type=f32)
    last = (((1,), (1,)), ((), ()))
    iota = lambda shape, dim: lax.broadcasted_iota(jnp.int32, shape, dim)
    pick = (iota((CELLS, SPECIES), 0) % SPECIES == iota((CELLS, SPECIES), 1)).astype(f32)
    source, target = iota((CELLS, CELLS), 0), iota((CELLS, CELLS), 1)
    same_row = source // SPECIES == target // SPECIES
    same_species = source % SPECIES == target % SPECIES
    diffusion = exact(diff_ref[...], pick, last)

    def tiled(matrix):
        return jnp.where(same_row, exact(exact(pick, matrix, last), pick, last), 0.0)

    def stencil(offset, middle):
        value = jnp.where(offset == 0, middle, 0.0)
        value = value + jnp.where((offset == 1) | (offset == -1), TAPS[1], 0.0)
        return value + jnp.where((offset == 2) | (offset == -2), TAPS[0], 0.0)

    def put(into, at, value):
        high_part = value.astype(bf16)
        into[:CELLS, at : at + CELLS] = high_part
        into[CELLS : 2 * CELLS, at : at + CELLS] = high_part
        into[2 * CELLS :, at : at + CELLS] = (value - high_part.astype(f32)).astype(bf16)

    offset = source // SPECIES - target // SPECIES
    spread = jnp.where(same_species, stencil(offset, 2.0 * TAPS[2]) * diffusion[0:1], 0.0)
    put(main_ref, 0, tiled(lin_ref[...]) + spread)
    put(main_ref, CELLS, tiled(coup_ref[...]))
    row_from = (source // SPECIES) % 2 + jnp.where(source < HALF, -2, ROWS)
    row_to = (target // SPECIES) % 2 + jnp.where(target < HALF, 0, ROWS - 2)
    alike = same_species & (source // EDGE == target // EDGE)
    put(edge_ref, 0, jnp.where(alike, stencil(row_from - row_to, 0.0) * diffusion[0:1], 0.0))
    diff_out[...] = diffusion * (1.0 / 12.0)


def make_weights(diffusion, linear_rates, coupling):
    return pl.pallas_call(
        weights_kernel,
        out_shape=[
            pltpu.VMEM((3 * CELLS, 2 * CELLS), bf16),
            pltpu.VMEM((3 * CELLS, CELLS), bf16),
            pltpu.VMEM((8, CELLS), f32),
        ],
        in_specs=[vmem()] * 3,
        out_specs=[vmem()] * 3,
        compiler_params=params(),
        name="weights",
    )(linear_rates, coupling, jnp.broadcast_to(diffusion[None], (8, SPECIES)))


def join_kernel(parts, out_ref, turn, whole, sem):
    copies = []
    for half in range(2):
        for slot in range(NCOL // 128):
            chunk, i = divmod(slot, CHUNK // 128)
            turn[slot] = parts[chunk, i * 128 : (i + 1) * 128, half * HALF : (half + 1) * HALF].T
            columns = slice(slot * 128, (slot + 1) * 128)
            for species in range(SPECIES):
                whole[half, species, :, columns] = turn[slot, pl.ds(species, ROWS // 2, stride=SPECIES), :]
        target = out_ref.at[:, half * (ROWS // 2) : (half + 1) * (ROWS // 2), :]
        copies.append(pltpu.make_async_copy(whole.at[half], target, sem.at[half]))
        copies[-1].start()
    for copy in copies:
        copy.wait()


def join(parts):
    return pl.pallas_call(
        join_kernel,
        out_shape=jax.ShapeDtypeStruct((SPECIES, ROWS, NCOL), f32),
        in_specs=[vmem()],
        out_specs=hbm(),
        scratch_shapes=[
            pltpu.VMEM((NCOL // 128, HALF, 128), f32),
            pltpu.VMEM((2, SPECIES, ROWS // 2, NCOL), f32),
            pltpu.SemaphoreType.DMA((2,)),
        ],
        compiler_params=params(),
        name="join",
    )(parts)


def after(value, *earlier):
    return lax.optimization_barrier((value, *earlier))[0]


WAVES = ((4, 1, 3), (2, 5), (6, 7))


def local(level_state, history, diffusion, linear_rates, coupling):
    state = level_state.reshape(CELLS, NCOL)
    hist = history.reshape(3, CELLS, NCOL)
    weights = make_weights(diffusion, linear_rates, coupling)
    first, lasts = cut(state, hist)
    fields = everyone(first)
    u = fields
    inner, outer = first_edges(fields)
    older = []
    got = {0: lasts[0]}
    edge = inner
    for step, n_out in enumerate((3, 2, 1, 0)):
        outer = send(outer, chip_swap())
        inner = send(inner, core_swap())
        earlier = list(got.values()) if step else [fields, edge]
        if step < 3:
            for by in WAVES[step]:
                got[by] = send(after(lasts[by], *earlier), level_swap(by))
        rate = inner_rates(step, after(u, *earlier) if step else u, weights)
        if step == 2:
            fields = gather([got[by] for by in range(LEVELS)])
        u, inner, outer, older = one_step(step, u, rate, inner, outer, weights, fields, older, n_out)
    return join(everyone(u))[None]


def solution(mesh):
    placed = (P("level", None, "tile", None), P("level", None, None, "tile", None), P(), P(), P())
    return jax.shard_map(
        local, mesh=mesh, in_specs=placed, out_specs=P("level", None, "tile", None), check_vma=False
    )
```

```python
import functools

import jax
import jax.numpy as jnp
from jax import lax
from jax.experimental import pallas as pl
from jax.experimental.pallas import tpu as pltpu
from jax.sharding import PartitionSpec as P

SPECIES = 16
ROWS = 16
CELLS = SPECIES * ROWS
HALF = CELLS // 2
NCOL = 2048
LEVELS = 8
CHUNK = NCOL // LEVELS
HALO = 8
WIDE = CHUNK + 2 * HALO
EDGE = 2 * SPECIES
STEP = 0.4
W0, W1, W2, W3 = (1.0 / 24.0, -5.0 / 24.0, 19.0 / 24.0, 9.0 / 24.0)
TAPS = (-1.0 / 12.0, 16.0 / 12.0, -30.0 / 12.0, 16.0 / 12.0, -1.0 / 12.0)
PAD = 8
FIELDS = 4
GROUP = HALF // EDGE
BAND = WIDE // 2

f32 = jnp.float32
bf16 = jnp.bfloat16
dot = functools.partial(jnp.dot, preferred_element_type=f32)


def params(mib=24, **kw):
    return pltpu.CompilerParams(vmem_limit_bytes=mib * 1024 * 1024, **kw)


def vmem():
    return pl.BlockSpec(memory_space=pltpu.VMEM)


def hbm():
    return pl.BlockSpec(memory_space=pl.ANY)


def core_swap():
    return [(l * 16 + t, l * 16 + (t ^ 1)) for l in range(LEVELS) for t in range(16)]


def chip_swap():
    return [(l * 16 + t, l * 16 + (t + (1 if t % 2 else 15)) % 16) for l in range(LEVELS) for t in range(16)]


def level_swap(by):
    return [(l * 16 + t, (l ^ by) * 16 + t) for l in range(LEVELS) if l ^ by < LEVELS for t in range(16)]


def send(value, pairs):
    return lax.ppermute(value, ("level", "tile"), pairs)


def everyone(value):
    return lax.all_to_all(value, "level", 0, 0)


def on_first_core():
    return lax.rem(lax.axis_index("tile"), 2) == 0


def cut_kernel(state_hbm, hist_hbm, out_ref, *refs):
    lasts, (state, hist, tiles, turned, in_sem, out_sem) = refs[:LEVELS], refs[LEVELS:]
    loads = [pltpu.make_async_copy(state_hbm, state, in_sem.at[0])]
    loads += [pltpu.make_async_copy(hist_hbm.at[n], hist.at[n], in_sem.at[n + 1]) for n in range(3)]
    for load in loads:
        load.start()

    def turn(n, value):
        tiles[n] = value
        rows = [tiles[n, pl.ds(row, SPECIES, stride=ROWS), :] for row in range(ROWS)]
        return jnp.concatenate(rows, axis=0).T

    def put(n, chunk, half, value):
        start = n * WIDE
        out_ref[chunk, start + HALO + half * 128 : start + HALO + (half + 1) * 128, :] = value
        if half == 0:
            other = lax.rem(chunk + LEVELS - 1, LEVELS)
            out_ref[other, start + WIDE - HALO : start + WIDE, :] = value[:HALO]
        else:
            other = lax.rem(chunk + 1, LEVELS)
            out_ref[other, start : start + HALO, :] = value[128 - HALO :]

    def columns(chunk, half):
        return pl.ds(pl.multiple_of(chunk * CHUNK + half * 128, 128), 128)

    def last_body(i, _):
        for half in range(2):
            r = hist[2, :, columns(i, half)]
            at = pl.multiple_of(i * CHUNK + half * 128 + HALO, 8)
            turned[pl.ds(at, 128), :] = turn(3, (STEP * W0) * r)
        return 0

    def state_body(chunk, _):
        for half in range(2):
            put(0, chunk, half, turn(0, state[:, columns(chunk, half)]))
        return 0

    def hist_body(chunk, _):
        for half in range(2):
            p, q, r = (hist[n, :, columns(chunk, half)] for n in range(3))
            put(1, chunk, half, turn(1, STEP * (W0 * p + W1 * q + (W2 - 1.0) * r)))
            put(2, chunk, half, turn(2, STEP * (W0 * q + W1 * r)))
        return 0

    loads[0].wait()
    lax.fori_loop(0, LEVELS, state_body, 0)
    for load in loads[1:]:
        load.wait()
    lax.fori_loop(0, LEVELS, last_body, 0)
    turned[:HALO, :] = turned[NCOL : NCOL + HALO, :]
    turned[NCOL + HALO :, :] = turned[HALO : 2 * HALO, :]
    copies = []
    for by, last_ref in enumerate(lasts):
        base = pl.multiple_of(lax.bitwise_xor(lax.axis_index("level"), by) * CHUNK, 128)
        copies.append(pltpu.make_async_copy(turned.at[pl.ds(base, WIDE), :], last_ref, out_sem.at[by]))
        copies[-1].start()
    lax.fori_loop(0, LEVELS, hist_body, 0)
    for copy in copies:
        copy.wait()


def cut(state, hist):
    outs = pl.pallas_call(
        cut_kernel,
        out_shape=[pltpu.VMEM((LEVELS, 3 * WIDE, CELLS), f32)] + [jax.ShapeDtypeStruct((WIDE, CELLS), f32)] * LEVELS,
        in_specs=[hbm()] * 2,
        out_specs=[vmem()] + [hbm()] * LEVELS,
        scratch_shapes=[
            pltpu.VMEM((CELLS, NCOL), f32),
            pltpu.VMEM((3, CELLS, NCOL), f32),
            pltpu.VMEM((FIELDS, CELLS, 128), f32),
            pltpu.VMEM((NCOL + 2 * HALO, CELLS), f32),
            pltpu.SemaphoreType.DMA((4,)),
            pltpu.SemaphoreType.DMA((LEVELS,)),
        ],
        compiler_params=params(54),
        name="cut",
    )(state, hist)
    return outs[0], outs[1:]


def gather_kernel(*refs):
    parts, out_ref, sem = refs[:LEVELS], refs[LEVELS], refs[LEVELS + 1]
    copies = []
    for by, part in enumerate(parts):
        level = lax.bitwise_xor(lax.axis_index("level"), by)
        copies.append(pltpu.make_async_copy(part, out_ref.at[level], sem.at[by]))
        copies[-1].start()
    for copy in copies:
        copy.wait()


def gather(parts):
    return pl.pallas_call(
        gather_kernel,
        out_shape=pltpu.VMEM((LEVELS, WIDE, CELLS), f32),
        in_specs=[hbm()] * LEVELS,
        out_specs=vmem(),
        scratch_shapes=[pltpu.SemaphoreType.DMA((LEVELS,))],
        compiler_params=params(),
        name="gather",
    )(*parts)


def pack_edges(u_ref, inner_ref, outer_ref):
    lane = lax.broadcasted_iota(jnp.int32, (BAND, HALF), 1)
    first_core = on_first_core()
    for group in range(LEVELS // GROUP):
        at = slice(group * HALF, (group + 1) * HALF)
        for begin in range(0, WIDE, BAND):
            rows = slice(begin, begin + BAND)
            down = up = None
            for k in range(GROUP):
                here = (lane >= k * EDGE) & (lane < (k + 1) * EDGE)
                top = u_ref[group * GROUP + k, rows, :HALF]
                bottom = u_ref[group * GROUP + k, rows, HALF:]
                top = pltpu.roll(top, k * EDGE, 1) if k else top
                bottom = pltpu.roll(bottom, (k + 1) * EDGE, 1) if k < GROUP - 1 else bottom
                down = top if k == 0 else jnp.where(here, top, down)
                up = bottom if k == 0 else jnp.where(here, bottom, up)
            inner_ref[rows, at] = jnp.where(first_core, up, down)
            outer_ref[rows, at] = jnp.where(first_core, down, up)


def edges_kernel(fields_ref, inner_ref, outer_ref):
    pack_edges(fields_ref, inner_ref, outer_ref)


HALO_SHAPE = jax.ShapeDtypeStruct((WIDE, LEVELS * EDGE), f32)


def first_edges(fields):
    return pl.pallas_call(
        edges_kernel,
        out_shape=[HALO_SHAPE] * 2,
        in_specs=[vmem()],
        out_specs=[vmem()] * 2,
        compiler_params=params(),
        name="edges",
    )(fields)


def split(into, at, value, rows=slice(0, WIDE)):
    high_part = value.astype(bf16)
    width = value.shape[1]
    into[rows, at : at + width] = high_part
    into[rows, CELLS + at : CELLS + at + width] = (value - high_part.astype(f32)).astype(bf16)
    into[rows, 2 * CELLS + at : 2 * CELLS + at + width] = high_part


def inner_kernel(u_ref, main_ref, diff_ref, rate_ref, padded, stack):
    padded[:, :, :PAD, :] = jnp.zeros((2, 2, PAD, HALF), f32)
    padded[:, :, PAD + WIDE :, :] = jnp.zeros((2, 2, PAD, HALF), f32)
    for pair in range(LEVELS // 2):
        for k in range(2):
            for side in range(2):
                part = u_ref[2 * pair + k, :WIDE, side * HALF : (side + 1) * HALF]
                padded[k, side, PAD : PAD + WIDE, :] = part
                split(stack, side * HALF, part, slice(k * WIDE, (k + 1) * WIDE))
        products = dot(stack[...], main_ref[...])
        for k in range(2):
            for side in range(2):
                at = slice(side * HALF, (side + 1) * HALF)
                diff = diff_ref[0:1, at]
                for begin in range(0, WIDE, BAND):
                    moved = lambda by: padded[k, side, PAD + begin + by : PAD + begin + by + BAND, :]
                    rows = slice(k * WIDE + begin, k * WIDE + begin + BAND)
                    u = moved(0)
                    near = moved(-1) + moved(1)
                    far = moved(-2) + moved(2)
                    rate = products[rows, at] + diff * (16.0 * near - far)
                    rate = rate + jnp.tanh(products[rows, CELLS + side * HALF : CELLS + (side + 1) * HALF])
                    rate_ref[2 * pair + k, begin : begin + BAND, at] = rate - u * u * u * (1.0 / 3.0)


def inner_rates(step, u, weights):
    main, _, diff = weights
    return pl.pallas_call(
        inner_kernel,
        out_shape=pltpu.VMEM((LEVELS, WIDE, CELLS), f32),
        in_specs=[vmem()] * 3,
        out_specs=vmem(),
        scratch_shapes=[
            pltpu.VMEM((2, 2, WIDE + 2 * PAD, HALF), f32),
            pltpu.VMEM((2 * WIDE, 3 * CELLS), bf16),
        ],
        compiler_params=params(),
        name=f"inner_{step}",
    )(u, main, diff)


def step_kernel(step, n_in, n_out, u_ref, rate_ref, inner_ref, outer_ref, edge_ref, *refs):
    refs = list(refs)
    take = lambda n: [refs.pop(0) for _ in range(n)]
    fields_ref = take(1)[0] if step < 3 else None
    older = take(n_in)
    next_ref = take(1)[0]
    sends = take(2) if step < 3 else None
    newer = take(n_out)
    stack, edges = take(2)
    first_core = on_first_core()
    for group in range(LEVELS // GROUP):
        at = slice(group * HALF, (group + 1) * HALF)
        inner, outer = inner_ref[:, at], outer_ref[:, at]
        split(stack, 0, jnp.where(first_core, outer, inner))
        split(stack, HALF, jnp.where(first_core, inner, outer))
        edges[group] = dot(stack[...], edge_ref[...])
    lane = lax.broadcasted_iota(jnp.int32, (BAND, HALF), 1)
    for side in range(2):
        at = slice(side * HALF, (side + 1) * HALF)
        near_edge = lane >= HALF - EDGE if side else lane < EDGE
        for begin in range(0, WIDE, BAND):
            rows = slice(begin, begin + BAND)
            below = None
            for level in range(LEVELS):
                group, k = divmod(level, GROUP)
                turn = (HALF - EDGE - k * EDGE if side else HALF - k * EDGE) % HALF
                edge = edges[group, rows, at]
                edge = pltpu.roll(edge, turn, 1) if turn else edge
                scaled = STEP * (rate_ref[level, rows, at] + jnp.where(near_edge, edge, 0.0))
                value = u_ref[level, rows, at] + scaled
                value = value if below is None else value + below
                if step < 3:
                    next_ref[level, rows, at] = value
                else:
                    low, high = max(begin, HALO), min(begin + BAND, HALO + CHUNK)
                    next_ref[level, low - HALO : high - HALO, at] = value[low - begin : high - begin]
                below = W3 * scaled
                if n_in > 0:
                    below = below + older[0][level, rows, at]
                if step < 3:
                    start = (0 if step == 2 else (step + 1) * WIDE) + begin
                    below = below + fields_ref[level, start : start + BAND, at]
                for i, weight in zip(range(n_out), (W2 - 1.0, W1, W0)):
                    value = weight * scaled
                    if i + 1 < n_in:
                        value = value + older[i + 1][level, rows, at]
                    newer[i][level, rows, at] = value
    if step < 3:
        pack_edges(next_ref, *sends)


def one_step(step, u, rate, inner, outer, weights, fields, older, n_out):
    n_in = len(older)
    full = pltpu.VMEM((LEVELS, WIDE, CELLS), f32)
    operands = [u, rate, inner, outer, weights[1]] + ([fields] if step < 3 else []) + older
    state = full if step < 3 else pltpu.VMEM((LEVELS, CHUNK, CELLS), f32)
    outs = [state] + ([HALO_SHAPE] * 2 if step < 3 else []) + [full] * n_out
    outs = pl.pallas_call(
        functools.partial(step_kernel, step, n_in, n_out),
        out_shape=outs,
        in_specs=[vmem()] * len(operands),
        out_specs=[vmem()] * len(outs),
        scratch_shapes=[
            pltpu.VMEM((WIDE, 3 * CELLS), bf16),
            pltpu.VMEM((LEVELS // GROUP, WIDE, CELLS), f32),
        ],
        compiler_params=params(),
        name=f"step_{step}",
    )(*operands)
    if step < 3:
        return outs[0], outs[1], outs[2], list(outs[3:])
    return outs[0], None, None, []


def weights_kernel(lin_ref, coup_ref, diff_ref, main_ref, edge_ref, diff_out):
    exact = functools.partial(lax.dot_general, precision=lax.Precision.HIGHEST, preferred_element_type=f32)
    last = (((1,), (1,)), ((), ()))
    iota = lambda shape, dim: lax.broadcasted_iota(jnp.int32, shape, dim)
    pick = (iota((CELLS, SPECIES), 0) % SPECIES == iota((CELLS, SPECIES), 1)).astype(f32)
    source, target = iota((CELLS, CELLS), 0), iota((CELLS, CELLS), 1)
    same_row = source // SPECIES == target // SPECIES
    same_species = source % SPECIES == target % SPECIES
    diffusion = exact(diff_ref[...], pick, last)

    def tiled(matrix):
        return jnp.where(same_row, exact(exact(pick, matrix, last), pick, last), 0.0)

    def stencil(offset, middle):
        value = jnp.where(offset == 0, middle, 0.0)
        value = value + jnp.where((offset == 1) | (offset == -1), TAPS[1], 0.0)
        return value + jnp.where((offset == 2) | (offset == -2), TAPS[0], 0.0)

    def put(into, at, value):
        high_part = value.astype(bf16)
        into[:CELLS, at : at + CELLS] = high_part
        into[CELLS : 2 * CELLS, at : at + CELLS] = high_part
        into[2 * CELLS :, at : at + CELLS] = (value - high_part.astype(f32)).astype(bf16)

    offset = source // SPECIES - target // SPECIES
    spread = jnp.where(same_species, stencil(offset, 2.0 * TAPS[2]) * diffusion[0:1], 0.0)
    put(main_ref, 0, tiled(lin_ref[...]) + spread)
    put(main_ref, CELLS, tiled(coup_ref[...]))
    row_from = (source // SPECIES) % 2 + jnp.where(source < HALF, -2, ROWS)
    row_to = (target // SPECIES) % 2 + jnp.where(target < HALF, 0, ROWS - 2)
    alike = same_species & (source // EDGE == target // EDGE)
    put(edge_ref, 0, jnp.where(alike, stencil(row_from - row_to, 0.0) * diffusion[0:1], 0.0))
    diff_out[...] = diffusion * (1.0 / 12.0)


def make_weights(diffusion, linear_rates, coupling):
    return pl.pallas_call(
        weights_kernel,
        out_shape=[
            pltpu.VMEM((3 * CELLS, 2 * CELLS), bf16),
            pltpu.VMEM((3 * CELLS, CELLS), bf16),
            pltpu.VMEM((8, CELLS), f32),
        ],
        in_specs=[vmem()] * 3,
        out_specs=[vmem()] * 3,
        compiler_params=params(),
        name="weights",
    )(linear_rates, coupling, jnp.broadcast_to(diffusion[None], (8, SPECIES)))


def join_kernel(parts, out_ref, turn, whole, sem):
    copies = []
    for half in range(2):
        for slot in range(NCOL // 128):
            chunk, i = divmod(slot, CHUNK // 128)
            turn[slot] = parts[chunk, i * 128 : (i + 1) * 128, half * HALF : (half + 1) * HALF].T
            columns = slice(slot * 128, (slot + 1) * 128)
            for species in range(SPECIES):
                whole[half, species, :, columns] = turn[slot, pl.ds(species, ROWS // 2, stride=SPECIES), :]
        target = out_ref.at[:, half * (ROWS // 2) : (half + 1) * (ROWS // 2), :]
        copies.append(pltpu.make_async_copy(whole.at[half], target, sem.at[half]))
        copies[-1].start()
    for copy in copies:
        copy.wait()


def join(parts):
    return pl.pallas_call(
        join_kernel,
        out_shape=jax.ShapeDtypeStruct((SPECIES, ROWS, NCOL), f32),
        in_specs=[vmem()],
        out_specs=hbm(),
        scratch_shapes=[
            pltpu.VMEM((NCOL // 128, HALF, 128), f32),
            pltpu.VMEM((2, SPECIES, ROWS // 2, NCOL), f32),
            pltpu.SemaphoreType.DMA((2,)),
        ],
        compiler_params=params(),
        name="join",
    )(parts)


def after(value, *earlier):
    return lax.optimization_barrier((value, *earlier))[0]


WAVES = ((4, 1, 3), (6, 5), (2, 7))


def local(level_state, history, diffusion, linear_rates, coupling):
    state = level_state.reshape(CELLS, NCOL)
    hist = history.reshape(3, CELLS, NCOL)
    weights = make_weights(diffusion, linear_rates, coupling)
    first, lasts = cut(state, hist)
    fields = everyone(first)
    u = fields
    inner, outer = first_edges(fields)
    older = []
    got = {0: lasts[0]}
    edge = inner
    for step, n_out in enumerate((3, 2, 1, 0)):
        outer = send(outer, chip_swap())
        inner = send(inner, core_swap())
        earlier = list(got.values()) if step else [fields, edge]
        if step < 3:
            for by in WAVES[step]:
                got[by] = send(after(lasts[by], *earlier), level_swap(by))
        rate = inner_rates(step, after(u, *earlier) if step else u, weights)
        if step == 2:
            fields = gather([got[by] for by in range(LEVELS)])
        u, inner, outer, older = one_step(step, u, rate, inner, outer, weights, fields, older, n_out)
    return join(everyone(u))[None]


def solution(mesh):
    placed = (P("level", None, "tile", None), P("level", None, None, "tile", None), P(), P(), P())
    return jax.shard_map(
        local, mesh=mesh, in_specs=placed, out_specs=P("level", None, "tile", None), check_vma=False
    )
```
